128 devices in a mesh: ctx: 8 (over y, core), head: 16 (over x, z).
Axes of the slice: x: 4, y: 4, z: 4, core: 2. Of those that a mesh axis runs over, the one named last changes fastest.
Arguments:
- queries: bfloat16 [4096, 16384], P('ctx', 'head'), may hold values from -8 to 8
- prompt_keys: bfloat16 [4096, 1024], P('ctx'), may hold values from -8 to 8
- prompt_values: bfloat16 [4096, 1024], P('ctx'), may hold values from -6 to 6
- owner_map: int32 [32, 8, 1], P('ctx'), may hold values from 0 to 15; in each aligned block of 32 rows (0 to 31, 32 to 63, ..., all dimensions but the last counted through in order) at most 4 rows name the same one
- head_layout: int32 [8], replicated, may hold values from 0 to 7, each once
- prompt_length: int32 [1], replicated, may hold values from 3840 to 4096
Outputs:
- attention: bfloat16 [4096, 16384], P('ctx', 'head')
- key_cache: bfloat16 [8, 64, 128, 128], P('ctx', 'head')
- value_cache: bfloat16 [8, 64, 128, 128], P('ctx', 'head')
- key_cache_scales: bfloat16 [8, 64], P('ctx', 'head')
- value_cache_scales: bfloat16 [8, 64], P('ctx', 'head')
The draws below stay inside these ranges and needn't reach their ends.
Inputs may be any that keep to these rules, and one draw needn't show every extreme that they name: `owner_map`: among the 32 entries of one block of 4 pages no owner appears more than 4 times, and in every draw some owner of some block appears exactly 4 times. `head_layout`: each key-value head appears once. `prompt_length`: positions from the prompt length on are padding.
All inputs are finite; a program needn't handle non-finite values.
Results may differ from the reference program's by a relative error of at most 0.04.
Values may be sent and summed in bfloat16 or wider, within the bound.
A program may use at most 64 MiB of HBM per device.

```python
import math
import jax
import jax.numpy as jnp
import numpy as np
from jax import lax

HEADS = 128
KVH = 8
HD = 128
PAGE = 128
TOK_DEV = 512
PROMPT = 4096
PAGE_DEV = 4
PAGES = 32
CTX_BLOCKS = 8
OWNERS = 16
SLOTS = 4


def draw_queries(key, part):
    own_key = jax.random.fold_in(key, 1)
    drawn = jnp.clip(jax.random.normal(own_key, (PROMPT, HEADS, HD), jnp.float32), -6.0, 6.0)
    return drawn.reshape(PROMPT, HEADS * HD).astype(jnp.bfloat16)


def draw_prompt_keys(key, part):
    own_key = jax.random.fold_in(key, 2)
    drawn = jnp.clip(jax.random.normal(own_key, (PROMPT, KVH, HD), jnp.float32), -6.0, 6.0)
    return drawn.reshape(PROMPT, KVH * HD).astype(jnp.bfloat16)


def block_levels(stream_key, shape, shards, smallest, top_value):
    factor_of = 1.0
    for dim, shards_of in shards:
        steps = jax.random.uniform(jax.random.fold_in(jax.random.fold_in(stream_key, 6), dim), (shards_of,), jnp.float32, smallest / len(shards), top_value / len(shards))
        factor_of = factor_of * jnp.repeat(jnp.exp(steps), shape[dim] // shards_of).reshape((-1,) + (1,) * (len(shape) - 1 - dim))
    return factor_of


def deal_out(key, own, number, rows, number_of, top, limit, lean):
    order = jax.random.permutation(key, number_of)
    packed, usual = shares(number_of, rows * top, limit, lean, True), shares(number_of, rows * top, limit, lean, False)
    places = jnp.arange(number_of)

    def named(lengths, offset_by):
        used = int((lengths > 0).sum())
        fixed = max(1, used // 4)
        shifted = fixed + (places - fixed + offset_by * (used - fixed)) % max(1, number_of - fixed)
        return jnp.zeros((number_of,), jnp.int32).at[order[jnp.where(places < fixed, places, shifted)]].set(jnp.asarray(lengths, jnp.int32))

    lengths = jnp.where(number % 4 == 0, named(packed, number // 4), named(usual, number - number // 4 - 1))
    mixed = jax.random.permutation(jax.random.fold_in(own, 3), number_of)
    source_of, taker = mixed[0:number_of // 2 * 2:2], mixed[1:number_of // 2 * 2:2]
    slack = jnp.minimum(lengths[source_of] - 1, limit - lengths[taker]) // 2
    slack = jnp.where((source_of == order[0]) | (taker == order[0]) | (lengths[taker] == 0), 0, jnp.maximum(slack, 0))
    shifted = jax.random.randint(jax.random.fold_in(own, 4), (number_of // 2,), 0, 1 << 20) % (slack + 1)
    lengths = lengths.at[source_of].add(-shifted).at[taker].add(shifted)
    labels = jnp.searchsorted(jnp.cumsum(lengths), jnp.arange(rows * top), side="right").astype(jnp.int32)
    grid = labels.reshape(top, rows).T
    grid = grid[jax.random.permutation(jax.random.fold_in(own, 1), rows)]
    offset_by = jax.random.randint(jax.random.fold_in(own, 2), (rows, 1), 0, top)
    return jnp.take_along_axis(grid, (jnp.arange(top)[None, :] + offset_by) % top, axis=1)


def shares(number_of, total, reach, slope, full):
    weights = [(1 << 20) // math.isqrt(standing ** slope) + 1 for standing in range(1, number_of + 1)]
    largest = reach if full else min(reach, max(-(-total // number_of), total * weights[0] // sum(weights)))
    least = 1 if total - largest >= number_of - 1 else 0
    counts, rest = [largest] + [least] * (number_of - 1), total - largest - least * (number_of - 1)
    while rest > 0:
        movable = [i for i in range(1, number_of) if counts[i] < largest] or [i for i in range(1, number_of) if counts[i] < reach]
        whole, budget = sum([weights[i] for i in movable]), rest
        for i in movable:
            more = min(reach - counts[i], max(1, budget * weights[i] // whole), rest)
            counts[i] = counts[i] + more
            rest = rest - more
    return np.array(counts)


def centred(key, dims, scale, reach, pieces=(), held_as=jnp.bfloat16):
    result = jax.random.normal(key, dims, jnp.float32) * scale
    if len(pieces) > 0:
        result = block_levels(key, dims, pieces, -0.22, 0.18) * result
    return jnp.clip(result, min=-reach, max=reach).astype(held_as)


def setup_inputs(seed: int = 0) -> dict:
    arg_keys = jax.random.split(jax.random.key(seed), 7)
    queries = draw_queries(jax.random.fold_in(arg_keys[6], 71), 0)
    prompt_keys = draw_prompt_keys(jax.random.fold_in(arg_keys[6], 71), 0)
    prompt_values = centred(arg_keys[2], (PROMPT, KVH * HD), 1.0, 6.0, ((0, 8),))
    owner_map_keys = jax.random.split(jax.random.fold_in(arg_keys[3], 1), PAGES * KVH // (PAGE_DEV * KVH))
    owner_map_turns = jax.random.permutation(jax.random.fold_in(arg_keys[3], 3), PAGES * KVH // (PAGE_DEV * KVH))
    owner_map = jax.vmap(lambda own, number: deal_out(jax.random.fold_in(arg_keys[3], 2), own, number, PAGE_DEV * KVH, OWNERS, 1, SLOTS, 2))(owner_map_keys, owner_map_turns).reshape((PAGES, KVH, 1))
    head_layout = jax.random.permutation(arg_keys[4], KVH).astype(jnp.int32)
    prompt_length = jax.random.randint(arg_keys[5], (1,), PROMPT - TOK_DEV // 2, PROMPT + 1).astype(jnp.int32)
    return dict(queries=queries, prompt_keys=prompt_keys, prompt_values=prompt_values, owner_map=owner_map, head_layout=head_layout, prompt_length=prompt_length)


def hadamard(width):
    index_row = jnp.arange(width, dtype=jnp.int32)
    common = index_row[:, None] & index_row[None, :]
    parity = jnp.zeros((width, width), jnp.int32)
    for bit_level in range(width.bit_length() - 1):
        parity = parity + (common >> bit_level & 1)
    return (1.0 - 2.0 * (parity % 2).astype(jnp.float32)) / math.sqrt(width)

def quantize(rotated):
    largest = lax.optimization_barrier(jnp.max(jnp.abs(rotated), axis=(1, 2)))
    scales = (largest / 448.0 + 1e-06).astype(jnp.bfloat16)
    stored = (rotated / scales.astype(jnp.float32)[:, None, None]).astype(jnp.bfloat16)
    return (stored, scales)

def entry_slots(owners, head_layout, page_count, slot_count):
    kv_total = head_layout.shape[0]
    heads_range = jnp.arange(kv_total, dtype=jnp.int32)
    layout_rank = lax.optimization_barrier(jnp.sum(heads_range[:, None] * (head_layout[:, None] == heads_range[None, :]).astype(jnp.int32), axis=0)).astype(jnp.int32)
    order_key = (layout_rank[None, :] * page_count + jnp.arange(page_count, dtype=jnp.int32)[:, None]).reshape(-1)
    earlier = order_key[None, :] < order_key[:, None]
    same_owner = owners[..., :, None] == owners[..., None, :]
    slot_index = lax.optimization_barrier(jnp.sum(jnp.logical_and(same_owner, earlier).astype(jnp.int32), axis=-1)).astype(jnp.int32)
    return owners * slot_count + slot_index

def reference(queries, prompt_keys, prompt_values, owner_map, head_layout, prompt_length):
    length = prompt_length[0]
    rotation = hadamard(HD)
    positions = jnp.arange(PROMPT, dtype=jnp.int32)
    live_rows = positions < length
    group_size = HEADS // KVH

    def store_pages(source):
        kept_rows = jnp.where(live_rows[:, None], source.astype(jnp.float32), 0.0).reshape(PROMPT, KVH, HD)
        rotated = jnp.einsum('tgd,de->gte', kept_rows, rotation, precision=lax.Precision.HIGHEST)
        stored, scales = quantize(rotated.reshape(KVH * PAGES, PAGE, HD))
        return (stored, scales)
    key_stored, key_scale = store_pages(prompt_keys)
    value_stored, value_scale = store_pages(prompt_values)
    key_tokens = key_stored.reshape(KVH, PROMPT, HD)
    value_tokens = value_stored.reshape(KVH, PROMPT, HD)
    key_cols = jnp.repeat(key_scale.reshape(KVH, PAGES).astype(jnp.float32), PAGE, axis=1)
    value_cols = jnp.repeat(value_scale.reshape(KVH, PAGES).astype(jnp.float32), PAGE, axis=1)
    rotated_queries = jnp.einsum('thd,de->hte', queries.reshape(PROMPT, HEADS, HD).astype(jnp.float32), rotation, precision=lax.Precision.HIGHEST).astype(jnp.bfloat16)
    allowed = jnp.logical_and(positions[None, :] <= positions[:, None], positions[None, :] < length)

    def one_head(head_number):
        kv_group = head_number // group_size
        scores = jnp.dot(rotated_queries[head_number], key_tokens[kv_group].T, preferred_element_type=jnp.float32) * key_cols[kv_group][None, :] / math.sqrt(HD)
        masked = jnp.where(allowed, scores, -1e+30)
        row_max = lax.optimization_barrier(jnp.max(masked, axis=1, keepdims=True))
        exp_scores = jnp.where(allowed, jnp.exp(masked - row_max), 0.0)
        denominator = lax.optimization_barrier(jnp.sum(exp_scores, axis=1, keepdims=True))
        weights = (exp_scores * value_cols[kv_group][None, :]).astype(jnp.bfloat16)
        return jnp.dot(weights, value_tokens[kv_group], preferred_element_type=jnp.float32) / denominator
    rotated_out = lax.map(one_head, jnp.arange(HEADS, dtype=jnp.int32))
    unrotated = jnp.einsum('htd,de->the', rotated_out, rotation, precision=lax.Precision.HIGHEST)
    attention = jnp.where(live_rows[:, None, None], unrotated, 0.0).astype(jnp.bfloat16).reshape(PROMPT, HEADS * HD)
    owners = owner_map[:, :, 0].reshape(CTX_BLOCKS, PAGE_DEV * KVH)
    destination = entry_slots(owners, head_layout, PAGE_DEV, SLOTS)
    block_ids = jnp.arange(CTX_BLOCKS, dtype=jnp.int32)[:, None]

    def to_cache(stored, scales):
        pages = stored.reshape(KVH, CTX_BLOCKS, PAGE_DEV, PAGE, HD).transpose(1, 2, 0, 3, 4).reshape(CTX_BLOCKS, PAGE_DEV * KVH, PAGE, HD)
        page_scales = scales.reshape(KVH, CTX_BLOCKS, PAGE_DEV).transpose(1, 2, 0).reshape(CTX_BLOCKS, PAGE_DEV * KVH)
        cache = jnp.zeros((CTX_BLOCKS, OWNERS * SLOTS, PAGE, HD), jnp.bfloat16).at[block_ids, destination].set(pages)
        cache_scales = jnp.zeros((CTX_BLOCKS, OWNERS * SLOTS), jnp.bfloat16).at[block_ids, destination].set(page_scales)
        return (cache, cache_scales)
    key_cache, key_cache_scales = to_cache(key_stored, key_scale)
    value_cache, value_cache_scales = to_cache(value_stored, value_scale)
    return (attention, key_cache, value_cache, key_cache_scales, value_cache_scales)
```

```python
import math

import jax
import jax.numpy as jnp
from jax import lax
from jax.experimental import pallas as pl
from jax.experimental.pallas import tpu as pltpu
from jax.sharding import PartitionSpec as P

HD = 128
PAGE = 128
TOK = 512
LH = 8
KVH = 8
PAGES = 4
SLOTS = 4
CHIPS = 4
MESH = pl.DeviceIdType.MESH
BF = jnp.bfloat16
F32 = jnp.float32
NEG = -1e30
LOGIT = math.log2(math.e) / math.sqrt(HD)


def dot(a, b, dims):
    return lax.dot_general(a, b, (dims, ((), ())), preferred_element_type=F32)


def qk(q, k):
    return dot(q, k, ((1,), (1,)))


def pv(p, v):
    return dot(p.astype(BF), v, ((1,), (0,)))


def wide(x, columns):
    return jnp.tile(x, (1, columns // x.shape[1]))


def signs():
    row = lax.broadcasted_iota(jnp.int32, (HD, HD), 0)
    column = lax.broadcasted_iota(jnp.int32, (HD, HD), 1)
    common = row & column
    parity = common & 1
    for bit in range(1, 7):
        parity = parity ^ ((common >> bit) & 1)
    return (1 - 2 * parity).astype(F32).astype(BF)


def kernel(
    q_hbm, pk_hbm, pv_hbm, owner_ref, layout_ref, length_ref,
    out_hbm, kc_hbm, vc_hbm, ks_ref, vs_ref,
    q_scr, pk_scr, pv_scr, kraw, kbuf, vbuf, acc, mx, out_scr, kc_scr, vc_scr,
    in_sem, out_sem, send_sem, recv_sem,
):
    c = lax.axis_index("ctx")
    head = lax.axis_index("head")
    y = c // 2
    k = c % 2
    g = head // 2
    sib = 2 * y + (1 - k)
    right = 2 * ((y + 1) % CHIPS) + k
    left = 2 * ((y + CHIPS - 1) % CHIPS) + k
    column = pl.ds(pl.multiple_of(g * HD, HD), HD)
    own_rows = pl.ds(pl.multiple_of(k * TOK, TOK), TOK)

    get_k = pltpu.make_async_copy(pk_hbm.at[:, column], kraw, in_sem.at[0])
    get_v = pltpu.make_async_copy(pv_hbm.at[:, column], vbuf.at[y, own_rows, pl.ds(0, HD)], in_sem.at[1])
    get_q = pltpu.make_async_copy(q_hbm, q_scr, in_sem.at[2])
    get_pk = pltpu.make_async_copy(pk_hbm, pk_scr, in_sem.at[3])
    get_pv = pltpu.make_async_copy(pv_hbm, pv_scr, in_sem.at[4])
    for copy in (get_k, get_v, get_q, get_pk, get_pv):
        copy.start()

    barrier = pltpu.get_barrier_semaphore()
    for other in (sib, left, right):
        pl.semaphore_signal(barrier, inc=1, device_id={"ctx": other}, device_id_type=MESH)

    get_k.wait()
    kbuf[y, own_rows, :] = (kraw[...].astype(F32) * LOGIT).astype(BF)
    get_v.wait()
    pl.semaphore_wait(barrier, 3)

    def block_refs(block):
        chip = block // 2
        rows = pl.ds(pl.multiple_of((block % 2) * TOK, TOK), TOK)
        return kbuf.at[chip, rows, :], vbuf.at[chip, rows, pl.ds(0, HD)]

    def copies(block, other, place):
        return [
            pltpu.make_async_remote_copy(
                src_ref=ref, dst_ref=ref, send_sem=send_sem.at[i, place], recv_sem=recv_sem.at[i, block],
                device_id={"ctx": other}, device_id_type=MESH,
            )
            for i, ref in enumerate(block_refs(block))
        ]

    def send(block, other, place):
        for copy in copies(block, other, place):
            copy.start()

    def sent(block, other, place):
        for copy in copies(block, other, place):
            copy.wait_send()

    def arrived(block):
        for copy in copies(block, sib, 0):
            copy.wait_recv()

    @pl.when(y < 3)
    def _():
        send(c, right, 0)

    @pl.when(y == 0)
    def _():
        send(c, left, 1)

    @pl.when(k == 0)
    def _():
        send(c, sib, 2)

    vbuf[:, :, HD:] = jnp.ones((CHIPS, 2 * TOK, HD), BF)

    length = length_ref[0]
    rotation = signs()
    found = jnp.int32(0)
    entry = [jnp.int32(-1)] * SLOTS
    for r in range(KVH):
        kv = layout_ref[r]
        for i in range(PAGES):
            owner = jnp.int32(0)
            for other in range(KVH):
                owner = jnp.where(kv == other, owner_ref[i * KVH + other], owner)
            mine = owner == head
            for s in range(SLOTS):
                entry[s] = jnp.where(mine & (found == s), i * KVH + kv, entry[s])
            found = found + jnp.where(mine, 1, 0)
    get_pk.wait()
    get_pv.wait()
    lanes = lax.broadcasted_iota(jnp.int32, (1, SLOTS), 1)
    page_row = lax.broadcasted_iota(jnp.int32, (PAGE, HD), 0)
    for source, cache, scale_ref in ((pk_scr, kc_scr, ks_ref), (pv_scr, vc_scr, vs_ref)):
        scale_row = jnp.zeros((1, SLOTS), F32)
        for s in range(SLOTS):
            raw = jnp.zeros((PAGE, HD), BF)
            for e in range(PAGES * KVH):
                page, kv = divmod(e, KVH)
                here = jnp.full((PAGE, HD), entry[s], jnp.int32) == e
                raw = jnp.where(here, source[page * PAGE : (page + 1) * PAGE, kv * HD : (kv + 1) * HD], raw)
            live = page_row + (c * TOK + (entry[s] >> 3) * PAGE) < length
            kept = jnp.where(live, raw.astype(F32), 0.0).astype(BF)
            rotated = dot(kept, rotation, ((1,), (0,))) * (1.0 / math.sqrt(HD))
            largest = jnp.max(jnp.max(jnp.abs(rotated), axis=1, keepdims=True), axis=0, keepdims=True)
            scale = (largest / 448.0 + 1e-6).astype(BF).astype(F32)
            stored = (rotated / scale).astype(BF).astype(F32)
            there = (jnp.zeros((1, 1), jnp.int32) + found) > s
            cache[s] = jnp.where(there, stored, 0.0).astype(BF)
            scale_row = jnp.where((lanes == s) & there, scale, scale_row)
        scale_ref[...] = scale_row.astype(BF)
    put_kc = pltpu.make_async_copy(kc_scr, kc_hbm.at[0], out_sem.at[0])
    put_vc = pltpu.make_async_copy(vc_scr, vc_hbm.at[0], out_sem.at[1])
    put_kc.start()
    put_vc.start()

    get_q.wait()

    def heads_q(h, rows=slice(None)):
        return q_scr[rows, h * HD : (h + 1) * HD]

    half = TOK // 2
    mask = lax.broadcasted_iota(jnp.int32, (half, half), 1) <= lax.broadcasted_iota(jnp.int32, (half, half), 0)
    k_own = kbuf[y, own_rows, :]
    v_own = vbuf[y, own_rows, :]
    for h in range(LH):
        for part in range(2):
            rows = slice(part * half, (part + 1) * half)
            s = qk(heads_q(h, rows), k_own[: (part + 1) * half])
            last = jnp.where(mask, s[:, part * half :], NEG)
            s = last if part == 0 else jnp.concatenate([s[:, :half], last], axis=1)
            m = jnp.broadcast_to(jnp.max(s, axis=1, keepdims=True), (half, HD))
            mx[h, rows, :] = m
            acc[h, rows, :] = pv(jnp.exp2(s - wide(m, s.shape[1])), v_own[: (part + 1) * half])

    def full(kb, vb):
        for h in range(LH):
            s = qk(heads_q(h), kb)
            old = mx[h]
            new = jnp.maximum(old, jnp.max(s, axis=1, keepdims=True))
            factor = jnp.exp2(old - new)
            mx[h] = new
            acc[h] = acc[h] * wide(factor, 2 * HD) + pv(jnp.exp2(s - wide(new, s.shape[1])), vb)

    @pl.when(k == 1)
    def _():
        arrived(sib)
        other_rows = pl.ds(0, TOK)
        full(kbuf[y, other_rows, :], vbuf[y, other_rows, :])

    def chip_of(t):
        return jnp.where(t == 0, y - 1, t - 1)

    def relays(t):
        return (t == 0) & ((y == 1) | (y == 2))

    def handle(t):
        block = 2 * chip_of(t) + k
        arrived(block)
        send(block, sib, 3 + t)

        @pl.when(relays(t))
        def _():
            send(block, right, 6)

    @pl.when(y > 0)
    def _():
        handle(0)

    def step(t, carry):
        @pl.when(t + 1 < y)
        def _():
            handle(t + 1)

        chip = chip_of(t)
        arrived(2 * chip + (1 - k))
        full(kbuf[chip], vbuf[chip])
        return carry

    lax.fori_loop(0, y, step, 0)

    row = lax.broadcasted_iota(jnp.int32, (TOK, HD), 0) + c * TOK
    for h in range(LH):
        o = acc[h, :, :HD] / acc[h, :, HD:]
        out_scr[:, h * HD : (h + 1) * HD] = jnp.where(row < length, o, 0.0).astype(BF)
    put_o = pltpu.make_async_copy(out_scr, out_hbm, out_sem.at[2])
    put_o.start()

    @pl.when(y < 3)
    def _():
        sent(c, right, 0)

    @pl.when(y == 0)
    def _():
        sent(c, left, 1)

    @pl.when(k == 0)
    def _():
        sent(c, sib, 2)

    def finish(t, carry):
        sent(2 * chip_of(t) + k, sib, 3 + t)

        @pl.when(relays(t))
        def _():
            sent(2 * chip_of(t) + k, right, 6)

        return carry

    lax.fori_loop(0, y, finish, 0)
    put_kc.wait()
    put_vc.wait()
    put_o.wait()


def per_device(queries, prompt_keys, prompt_values, owner_map, head_layout, prompt_length):
    any_ = pl.BlockSpec(memory_space=pl.ANY)
    smem = pl.BlockSpec(memory_space=pltpu.SMEM)
    vmem = pl.BlockSpec(memory_space=pltpu.VMEM)
    return pl.pallas_call(
        kernel,
        out_shape=(
            jax.ShapeDtypeStruct((TOK, LH * HD), BF),
            jax.ShapeDtypeStruct((1, SLOTS, PAGE, HD), BF),
            jax.ShapeDtypeStruct((1, SLOTS, PAGE, HD), BF),
            jax.ShapeDtypeStruct((1, SLOTS), BF),
            jax.ShapeDtypeStruct((1, SLOTS), BF),
        ),
        in_specs=[any_, any_, any_, smem, smem, smem],
        out_specs=(any_, any_, any_, vmem, vmem),
        scratch_shapes=[
            pltpu.VMEM((TOK, LH * HD), BF),
            pltpu.VMEM((TOK, KVH * HD), BF),
            pltpu.VMEM((TOK, KVH * HD), BF),
            pltpu.VMEM((TOK, HD), BF),
            pltpu.VMEM((CHIPS, 2 * TOK, HD), BF),
            pltpu.VMEM((CHIPS, 2 * TOK, 2 * HD), BF),
            pltpu.VMEM((LH, TOK, 2 * HD), F32),
            pltpu.VMEM((LH, TOK, HD), F32),
            pltpu.VMEM((TOK, LH * HD), BF),
            pltpu.VMEM((SLOTS, PAGE, HD), BF),
            pltpu.VMEM((SLOTS, PAGE, HD), BF),
            pltpu.SemaphoreType.DMA((5,)),
            pltpu.SemaphoreType.DMA((3,)),
            pltpu.SemaphoreType.DMA((2, 7)),
            pltpu.SemaphoreType.DMA((2, 8)),
        ],
        compiler_params=pltpu.CompilerParams(
            collective_id=0, has_side_effects=True, vmem_limit_bytes=56 << 20
        ),
        name="prefill",
    )(queries, prompt_keys, prompt_values, owner_map.reshape(-1), head_layout, prompt_length)


def solution(mesh):
    in_specs = (P("ctx", "head"), P("ctx", None), P("ctx", None), P("ctx", None, None), P(), P())
    out_specs = (
        P("ctx", "head"),
        P("ctx", "head", None, None),
        P("ctx", "head", None, None),
        P("ctx", "head"),
        P("ctx", "head"),
    )
    return jax.shard_map(
        per_device, mesh=mesh, in_specs=in_specs, out_specs=out_specs, check_vma=False
    )
```

```python
import math

import jax
import jax.numpy as jnp
from jax import lax
from jax.experimental import pallas as pl
from jax.experimental.pallas import tpu as pltpu
from jax.sharding import PartitionSpec as P

HD = 128
PAGE = 128
TOK = 512
LH = 8
KVH = 8
PAGES = 4
SLOTS = 4
CHIPS = 4
MESH = pl.DeviceIdType.MESH
HALF = TOK // 2
GIVEN = 0
BF = jnp.bfloat16
F32 = jnp.float32
NEG = -1e30
LOGIT = math.log2(math.e) / math.sqrt(HD)


def dot(a, b, dims):
    return lax.dot_general(a, b, (dims, ((), ())), preferred_element_type=F32)


def qk(q, k):
    return dot(q, k, ((1,), (1,)))


def pv(p, v):
    return dot(p.astype(BF), v, ((1,), (0,)))


def wide(x, columns):
    return jnp.tile(x, (1, columns // x.shape[1]))


def signs():
    row = lax.broadcasted_iota(jnp.int32, (HD, HD), 0)
    column = lax.broadcasted_iota(jnp.int32, (HD, HD), 1)
    common = row & column
    parity = common & 1
    for bit in range(1, 7):
        parity = parity ^ ((common >> bit) & 1)
    return (1 - 2 * parity).astype(F32).astype(BF)


def kernel(
    q_hbm, pk_hbm, pv_hbm, length_ref, out_ref,
    q_scr, store, acc, mx, fq, facc, fmx, fout,
    in_sem, own_sem, y_send, y_recv, s_send, s_recv, q_send, q_recv, o_send, o_recv,
):
    c = lax.axis_index("ctx")
    head = lax.axis_index("head")
    y = c // 2
    k = c % 2
    g = head // 2
    sib = {"ctx": 2 * y + (1 - k)}
    right = {"ctx": 2 * ((y + 1) % CHIPS) + k}
    left = {"ctx": 2 * ((y + CHIPS - 1) % CHIPS) + k}
    other_end = {"ctx": 7 - c}
    column = pl.ds(pl.multiple_of(g * HD, HD), HD)
    home = y == 3
    helper = y == 0
    inputs = (pk_hbm, pv_hbm)

    barrier = pltpu.get_barrier_semaphore()
    others = (sib, left, right, other_end) if GIVEN else (sib, left, right)
    for other in others:
        pl.semaphore_signal(barrier, inc=1, device_id=other, device_id_type=MESH)

    def piece(chip, parity, kind, a):
        return store.at[chip, kind, a, pl.ds(pl.multiple_of(parity * HALF, HALF), HALF), :]

    def raw(kind, a):
        return inputs[kind].at[pl.ds(a * HALF, HALF), column]

    def both(a):
        return ((0, a), (1, a))

    get_own = [
        pltpu.make_async_copy(raw(kind, a), piece(y, k, kind, a), own_sem.at[kind, a]) for a in range(2) for kind in range(2)
    ]
    get_q = pltpu.make_async_copy(q_hbm, q_scr, in_sem)
    for copy in (*get_own, get_q):
        copy.start()

    def remote(src, dst, send_sem, recv_sem, device):
        return pltpu.make_async_remote_copy(
            src_ref=src, dst_ref=dst, send_sem=send_sem, recv_sem=recv_sem, device_id=device, device_id_type=MESH
        )

    def own_over_y(a, device, place, act):
        for kind in range(2):
            act(remote(raw(kind, a), piece(y, k, kind, a), y_send.at[place, kind, a], y_recv.at[y, kind, a], device))

    def over_y(chip, a, device, place, act):
        for kind in range(2):
            ref = piece(chip, k, kind, a)
            act(remote(ref, ref, y_send.at[place, kind, a], y_recv.at[chip, kind, a], device))

    def own_over_core(act):
        for a in range(2):
            for kind in range(2):
                act(remote(raw(kind, a), piece(y, k, kind, a), s_send.at[y, kind, a], s_recv.at[y, kind, a], sib))

    def over_core(chip, parity, a, act):
        for kind in range(2):
            ref = piece(chip, parity, kind, a)
            act(remote(ref, ref, s_send.at[chip, kind, a], s_recv.at[chip, kind, a], sib))

    def ask(f):
        cols = pl.ds((LH - GIVEN + f) * HD, HD)
        return remote(q_hbm.at[:, cols], fq.at[f], q_send.at[f], q_recv.at[f], other_end)

    def give_back(f):
        cols = pl.ds((LH - GIVEN + f) * HD, HD)
        return remote(fout.at[f], out_ref.at[:, cols], o_send.at[f], o_recv.at[f], other_end)

    def start(copy):
        copy.start()

    def wait_recv(copy):
        copy.wait_recv()

    def wait_send(copy):
        copy.wait_send()

    chunks = jnp.where(helper, CHIPS - 1 if GIVEN else 0, y)

    def source(i):
        return jnp.where(helper, jnp.where(i == 0, 1, jnp.where(i == 1, 3, 2)), jnp.where(i == 0, y - 1, i - 1))

    def sends(a, act):
        @pl.when(y < (4 if GIVEN else 3))
        def _():
            own_over_y(a, right, 0, act)

        @pl.when(y < (3 if GIVEN else 1))
        def _():
            own_over_y(a, left, 1, act)

    def asks(act):
        if GIVEN:
            @pl.when(home)
            def _():
                for f in range(GIVEN):
                    act(ask(f))

    def core_sends(act):
        @pl.when((k == 0) | (helper & (GIVEN > 0)))
        def _():
            own_over_core(act)

    def forwards(i, a, act):
        over_core(source(i), k, a, act)

        @pl.when((i == 0) & ((y == 1) | (y == 2)))
        def _():
            over_y(source(i), a, right, 2, act)

    def first(i, a):
        over_y(source(i), a, right, 0, wait_recv)
        forwards(i, a, start)

    def third(i, a):
        over_core(source(i), 1 - k, a, wait_recv)

    pl.semaphore_wait(barrier, len(others))
    asks(start)
    sends(0, start)
    core_sends(start)

    length = length_ref[0]
    get_q.wait()
    q_scr[...] = (q_scr[...].astype(F32) * LOGIT).astype(BF)
    for copy in get_own:
        copy.wait()

    ones = jnp.ones((2 * TOK, HD), BF)

    def with_ones(v):
        return jnp.concatenate([v, ones[: v.shape[0]]], axis=1)

    mask = lax.broadcasted_iota(jnp.int32, (HALF, HALF), 1) <= lax.broadcasted_iota(jnp.int32, (HALF, HALF), 0)

    class Own:
        def __init__(self, h):
            self.h = h

        def q(self, rows=slice(None)):
            return q_scr[rows, self.h * HD : (self.h + 1) * HD]

        def state(self):
            return mx.at[self.h], acc.at[self.h]

    class Foreign:
        def __init__(self, f):
            self.f = f

        def q(self, rows=slice(None)):
            return fq[self.f, rows, :]

        def state(self):
            return fmx, facc

    def block(chip, kind, parity):
        rows = pl.ds(pl.multiple_of(parity * HALF, HALF), HALF)
        return jnp.concatenate([store[chip, kind, a, rows, :] for a in range(2)], axis=0)

    def chunk(chip, kind):
        return store[chip, kind].reshape(2 * TOK, HD)

    def causal(items, kb, vb):
        before = kb.shape[0] - TOK
        vb = with_ones(vb)
        for item in items:
            top, total = item.state()
            for part in range(2):
                rows = slice(part * HALF, (part + 1) * HALF)
                keys = before + (part + 1) * HALF
                s = qk(item.q(rows), kb[:keys])
                last = jnp.where(mask, s[:, keys - HALF :], NEG)
                s = last if keys == HALF else jnp.concatenate([s[:, : keys - HALF], last], axis=1)
                t = jnp.broadcast_to(jnp.max(s, axis=1, keepdims=True), (HALF, HD))
                top[rows, :] = t
                total[rows, :] = pv(jnp.exp2(s - wide(t, keys)), vb[:keys])

    def full(items, kb, vb):
        vb = with_ones(vb)
        for item in items:
            top, total = item.state()
            s = qk(item.q(), kb)
            old = top[...]
            new = jnp.maximum(old, jnp.max(s, axis=1, keepdims=True))
            factor = jnp.exp2(old - new)
            top[...] = new
            total[...] = total[...] * wide(factor, 2 * HD) + pv(jnp.exp2(s - wide(new, s.shape[1])), vb)

    own = [Own(h) for h in range(LH)]
    kept_heads = own[: LH - GIVEN]

    def on_own(condition, run):
        if GIVEN:
            pl.when(condition & home)(lambda: run(kept_heads))
            pl.when(condition & jnp.logical_not(home))(lambda: run(own))
        else:
            pl.when(condition)(lambda: run(own))

    on_own(c >= 0, lambda items: causal(items, block(y, 0, k), block(y, 1, k)))
    sends(1, start)

    @pl.when((k == 1) | (helper & (GIVEN > 0)))
    def _():
        for a in range(2):
            over_core(y, 1 - k, a, wait_recv)

    on_own(k == 1, lambda items: full(items, block(y, 0, 0), block(y, 1, 0)))

    near = y - 1
    two = (y == 3) | (helper & (GIVEN > 0))

    @pl.when(chunks > 0)
    def _():
        first(0, 0)

    @pl.when(two)
    def _():
        first(1, 0)

    @pl.when(chunks > 0)
    def _():
        third(0, 0)

    on_own(y > 0, lambda items: full(items, store[near, 0, 0], store[near, 1, 0]))

    @pl.when(chunks > 0)
    def _():
        first(0, 1)

    @pl.when(two)
    def _():
        first(1, 1)
        third(1, 0)

    on_own(y == 3, lambda items: full(items, store[0, 0, 0], store[0, 1, 0]))

    @pl.when(chunks > 0)
    def _():
        third(0, 1)

    on_own(y > 0, lambda items: full(items, store[near, 0, 1], store[near, 1, 1]))

    @pl.when(two)
    def _():
        for a in range(2):
            first(2, a)
        third(1, 1)

    on_own(y == 3, lambda items: full(items, store[0, 0, 1], store[0, 1, 1]))

    @pl.when(y == 2)
    def _():
        for a in range(2):
            first(1, a)
        for a in range(2):
            third(1, a)

    @pl.when(two)
    def _():
        for a in range(2):
            third(2, a)

    last = 3 - y + jnp.where(y == 3, 1, 0) - jnp.where(y == 2, 1, 0)
    on_own((y == 2) | (y == 3), lambda items: full(items, chunk(last, 0), chunk(last, 1)))

    row = lax.broadcasted_iota(jnp.int32, (TOK, HD), 0)

    def normal(total, position):
        o = total[:, :HD] / total[:, HD:]
        return jnp.where(row + position < length, o, 0.0).astype(BF)

    if GIVEN:
        @pl.when(helper)
        def _():
            for f in range(GIVEN):
                ask(f).wait_recv()
                fq[f] = (fq[f].astype(F32) * LOGIT).astype(BF)
                item = Foreign(f)

                @pl.when(k == 0)
                def _():
                    causal(
                        [item],
                        jnp.concatenate([block(3, 0, 0), block(3, 0, 1)], axis=0),
                        jnp.concatenate([block(3, 1, 0), block(3, 1, 1)], axis=0),
                    )

                @pl.when(k == 1)
                def _():
                    causal([item], block(3, 0, 0), block(3, 1, 0))

                for chip in (0, 1, 2):
                    full([item], chunk(chip, 0), chunk(chip, 1))
                fout[f] = normal(facc, (7 - c) * TOK)
                give_back(f).start()

    def finish(items):
        for item in items:
            out_ref[:, item.h * HD : (item.h + 1) * HD] = normal(acc.at[item.h], c * TOK)

    finish(kept_heads)
    if GIVEN:
        @pl.when(jnp.logical_not(home))
        def _():
            finish(own[LH - GIVEN :])

        @pl.when(home)
        def _():
            for f in range(GIVEN):
                give_back(f).wait_recv()

    asks(wait_send)
    for a in range(2):
        sends(a, wait_send)
    core_sends(wait_send)

    def done(i, carry):
        for a in range(2):
            forwards(i, a, wait_send)
        return carry

    lax.fori_loop(0, chunks, done, 0)

    if GIVEN:
        @pl.when(y == 1)
        def _():
            for a in range(2):
                over_y(2, a, left, 3, wait_send)

        @pl.when(helper)
        def _():
            for f in range(GIVEN):
                give_back(f).wait_send()


def hand_over(
    att_ref, pk_hbm, pv_hbm, owner_ref, layout_ref, length_ref,
    att, kc, vc, ks, vs,
    raw, made, b_ks, b_vs, att_sem, in_sem, out_sem,
):
    head = lax.axis_index("head")
    start = lax.axis_index("ctx") * TOK
    put = pltpu.make_async_copy(att_ref, att, att_sem)
    put.start()

    length = length_ref[0]
    found = jnp.int32(0)
    entry = [jnp.int32(0)] * SLOTS
    for r in range(KVH):
        kv = layout_ref[r]
        for i in range(PAGES):
            mine = owner_ref[i, 0, kv] == head
            for s in range(SLOTS):
                entry[s] = jnp.where(mine & (found == s), i * KVH + kv, entry[s])
            found = found + jnp.where(mine, 1, 0)
    gets = []
    for kind, source in enumerate((pk_hbm, pv_hbm)):
        for s in range(SLOTS):
            rows = pl.ds(pl.multiple_of((entry[s] >> 3) * PAGE, PAGE), PAGE)
            columns = pl.ds(pl.multiple_of((entry[s] & 7) * HD, HD), HD)
            gets.append(pltpu.make_async_copy(source.at[rows, columns], raw.at[kind, s], in_sem.at[kind, s]))
    for copy in gets:
        copy.start()
    rotation = signs()
    lanes = lax.broadcasted_iota(jnp.int32, (1, SLOTS), 1)
    page_row = lax.broadcasted_iota(jnp.int32, (PAGE, HD), 0)
    for copy in gets:
        copy.wait()
    puts = []
    for kind, (cache, scale_out, scale_scr) in enumerate(((kc, ks, b_ks), (vc, vs, b_vs))):
        kept = []
        for s in range(SLOTS):
            live = page_row + (start + (entry[s] >> 3) * PAGE) < length
            kept.append(jnp.where(live, raw[kind, s].astype(F32), 0.0).astype(BF))
        rotated = dot(jnp.concatenate(kept, axis=0), rotation, ((1,), (0,))) * (1.0 / math.sqrt(HD))
        rotated = rotated.reshape(SLOTS, PAGE, HD)
        largest = jnp.max(jnp.max(jnp.abs(rotated), axis=1, keepdims=True), axis=2, keepdims=True)
        scales = (largest / 448.0 + 1e-6).astype(BF).astype(F32)
        stored = rotated / scales
        scale_row = jnp.zeros((1, SLOTS), F32)
        for s in range(SLOTS):
            there = (jnp.zeros((1, 1), jnp.int32) + found) > s
            made[kind, s] = jnp.where(there, stored[s], 0.0).astype(BF)
            scale_row = jnp.where((lanes == s) & there, scales[s], scale_row)
        scale_scr[...] = scale_row.astype(BF)
        puts.append(pltpu.make_async_copy(made.at[kind], cache.at[0], out_sem.at[kind, 0]))
        puts.append(pltpu.make_async_copy(scale_scr, scale_out, out_sem.at[kind, 1]))
        for copy in puts[-2:]:
            copy.start()
    put.wait()
    for copy in puts:
        copy.wait()


def per_device(queries, prompt_keys, prompt_values, owner_map, head_layout, prompt_length):
    any_ = pl.BlockSpec(memory_space=pl.ANY)
    smem = pl.BlockSpec(memory_space=pltpu.SMEM)
    vmem = pl.BlockSpec(memory_space=pltpu.VMEM)
    dma = pltpu.SemaphoreType.DMA
    given = max(GIVEN, 1)
    attention = pl.pallas_call(
        kernel,
        out_shape=pltpu.VMEM((TOK, LH * HD), BF),
        in_specs=[any_, any_, any_, smem],
        out_specs=vmem,
        scratch_shapes=[
            pltpu.VMEM((TOK, LH * HD), BF),
            pltpu.VMEM((CHIPS, 2, 2, TOK, HD), BF),
            pltpu.VMEM((LH, TOK, 2 * HD), F32),
            pltpu.VMEM((LH, TOK, HD), F32),
            pltpu.VMEM((given, TOK, HD), BF),
            pltpu.VMEM((TOK, 2 * HD), F32),
            pltpu.VMEM((TOK, HD), F32),
            pltpu.VMEM((given, TOK, HD), BF),
            dma,
            dma((2, 2)),
            dma((4, 2, 2)),
            dma((CHIPS, 2, 2)),
            dma((CHIPS, 2, 2)),
            dma((CHIPS, 2, 2)),
            dma((given,)),
            dma((given,)),
            dma((given,)),
            dma((given,)),
        ],
        compiler_params=pltpu.CompilerParams(
            collective_id=0, has_side_effects=True, vmem_limit_bytes=56 << 20
        ),
        name="prefill",
    )(queries, prompt_keys, prompt_values, prompt_length)
    return pl.pallas_call(
        hand_over,
        out_shape=(
            jax.ShapeDtypeStruct((TOK, LH * HD), BF),
            jax.ShapeDtypeStruct((1, SLOTS, PAGE, HD), BF),
            jax.ShapeDtypeStruct((1, SLOTS, PAGE, HD), BF),
            jax.ShapeDtypeStruct((1, SLOTS), BF),
            jax.ShapeDtypeStruct((1, SLOTS), BF),
        ),
        in_specs=[vmem, any_, any_, smem, smem, smem],
        out_specs=(any_,) * 5,
        scratch_shapes=[
            pltpu.VMEM((2, SLOTS, PAGE, HD), BF),
            pltpu.VMEM((2, SLOTS, PAGE, HD), BF),
            pltpu.VMEM((1, SLOTS), BF),
            pltpu.VMEM((1, SLOTS), BF),
            dma,
            dma((2, SLOTS)),
            dma((2, 2)),
        ],
        compiler_params=pltpu.CompilerParams(vmem_limit_bytes=8 << 20),
        name="hand_over",
    )(attention, prompt_keys, prompt_values, owner_map.transpose(0, 2, 1), head_layout, prompt_length)


def solution(mesh):
    in_specs = (P("ctx", "head"), P("ctx", None), P("ctx", None), P("ctx", None, None), P(), P())
    out_specs = (
        P("ctx", "head"),
        P("ctx", "head", None, None),
        P("ctx", "head", None, None),
        P("ctx", "head"),
        P("ctx", "head"),
    )
    return jax.shard_map(
        per_device, mesh=mesh, in_specs=in_specs, out_specs=out_specs, check_vma=False
    )
```

```python
import math

import jax
import jax.numpy as jnp
from jax import lax
from jax.experimental import pallas as pl
from jax.experimental.pallas import tpu as pltpu
from jax.sharding import PartitionSpec as P

HD = 128
PAGE = 128
TOK = 512
LH = 8
KVH = 8
PAGES = 4
SLOTS = 4
CHIPS = 4
MESH = pl.DeviceIdType.MESH
HALF = TOK // 2
GIVEN = 1
BF = jnp.bfloat16
F32 = jnp.float32
NEG = -1e30
LOGIT = math.log2(math.e) / math.sqrt(HD)


def dot(a, b, dims):
    return lax.dot_general(a, b, (dims, ((), ())), preferred_element_type=F32)


def qk(q, k):
    return dot(q, k, ((1,), (1,)))


def pv(p, v):
    return dot(p.astype(BF), v, ((1,), (0,)))


def wide(x, columns):
    return jnp.tile(x, (1, columns // x.shape[1]))


def signs():
    row = lax.broadcasted_iota(jnp.int32, (HD, HD), 0)
    column = lax.broadcasted_iota(jnp.int32, (HD, HD), 1)
    common = row & column
    parity = common & 1
    for bit in range(1, 7):
        parity = parity ^ ((common >> bit) & 1)
    return (1 - 2 * parity).astype(F32).astype(BF)


def kernel(
    q_hbm, pk_hbm, pv_hbm, length_ref, out_ref,
    q_scr, store, acc, mx, fq, facc, fmx, fout,
    in_sem, own_sem, y_send, y_recv, s_send, s_recv, q_send, q_recv, o_send, o_recv,
):
    c = lax.axis_index("ctx")
    head = lax.axis_index("head")
    y = c // 2
    k = c % 2
    g = head // 2
    sib = {"ctx": 2 * y + (1 - k)}
    right = {"ctx": 2 * ((y + 1) % CHIPS) + k}
    left = {"ctx": 2 * ((y + CHIPS - 1) % CHIPS) + k}
    other_end = {"ctx": 7 - c}
    column = pl.ds(pl.multiple_of(g * HD, HD), HD)
    home = y == 3
    helper = y == 0
    inputs = (pk_hbm, pv_hbm)

    barrier = pltpu.get_barrier_semaphore()
    others = (sib, left, right, other_end) if GIVEN else (sib, left, right)
    for other in others:
        pl.semaphore_signal(barrier, inc=1, device_id=other, device_id_type=MESH)

    def piece(chip, parity, kind, a):
        return store.at[chip, kind, a, pl.ds(pl.multiple_of(parity * HALF, HALF), HALF), :]

    def raw(kind, a):
        return inputs[kind].at[pl.ds(a * HALF, HALF), column]

    def both(a):
        return ((0, a), (1, a))

    get_own = [
        pltpu.make_async_copy(raw(kind, a), piece(y, k, kind, a), own_sem.at[kind, a]) for a in range(2) for kind in range(2)
    ]
    get_q = pltpu.make_async_copy(q_hbm, q_scr, in_sem)
    for copy in (*get_own, get_q):
        copy.start()

    def remote(src, dst, send_sem, recv_sem, device):
        return pltpu.make_async_remote_copy(
            src_ref=src, dst_ref=dst, send_sem=send_sem, recv_sem=recv_sem, device_id=device, device_id_type=MESH
        )

    def own_over_y(a, device, place, act):
        for kind in range(2):
            act(remote(raw(kind, a), piece(y, k, kind, a), y_send.at[place, kind, a], y_recv.at[y, kind, a], device))

    def over_y(chip, a, device, place, act):
        for kind in range(2):
            ref = piece(chip, k, kind, a)
            act(remote(ref, ref, y_send.at[place, kind, a], y_recv.at[chip, kind, a], device))

    def own_over_core(act):
        for a in range(2):
            for kind in range(2):
                act(remote(raw(kind, a), piece(y, k, kind, a), s_send.at[y, kind, a], s_recv.at[y, kind, a], sib))

    def over_core(chip, parity, a, act):
        for kind in range(2):
            ref = piece(chip, parity, kind, a)
            act(remote(ref, ref, s_send.at[chip, kind, a], s_recv.at[chip, kind, a], sib))

    def ask(f):
        cols = pl.ds((LH - GIVEN + f) * HD, HD)
        return remote(q_hbm.at[:, cols], fq.at[f], q_send.at[f], q_recv.at[f], other_end)

    def give_back(f):
        cols = pl.ds((LH - GIVEN + f) * HD, HD)
        return remote(fout.at[f], out_ref.at[:, cols], o_send.at[f], o_recv.at[f], other_end)

    def start(copy):
        copy.start()

    def wait_recv(copy):
        copy.wait_recv()

    def wait_send(copy):
        copy.wait_send()

    chunks = jnp.where(helper, CHIPS - 1 if GIVEN else 0, y)

    def source(i):
        return jnp.where(helper, jnp.where(i == 0, 1, jnp.where(i == 1, 3, 2)), jnp.where(i == 0, y - 1, i - 1))

    def sends(a, act):
        @pl.when(y < (4 if GIVEN else 3))
        def _():
            own_over_y(a, right, 0, act)

        @pl.when(y < (3 if GIVEN else 1))
        def _():
            own_over_y(a, left, 1, act)

    def asks(act):
        if GIVEN:
            @pl.when(home)
            def _():
                for f in range(GIVEN):
                    act(ask(f))

    def core_sends(act):
        @pl.when((k == 0) | (helper & (GIVEN > 0)))
        def _():
            own_over_core(act)

    def forwards(i, a, act):
        over_core(source(i), k, a, act)

        @pl.when((i == 0) & ((y == 1) | (y == 2)))
        def _():
            over_y(source(i), a, right, 2, act)

    def passes(a):
        if GIVEN:
            @pl.when(y == 1)
            def _():
                over_y(2, a, left, 3, wait_recv)
                over_y(2, a, left, 3, start)

    def first(i, a):
        over_y(source(i), a, right, 0, wait_recv)
        forwards(i, a, start)

    def third(i, a):
        over_core(source(i), 1 - k, a, wait_recv)

    pl.semaphore_wait(barrier, len(others))
    asks(start)
    sends(0, start)
    core_sends(start)

    length = length_ref[0]
    get_q.wait()
    q_scr[...] = (q_scr[...].astype(F32) * LOGIT).astype(BF)
    for copy in get_own:
        copy.wait()

    ones = jnp.ones((2 * TOK, HD), BF)

    def with_ones(v):
        return jnp.concatenate([v, ones[: v.shape[0]]], axis=1)

    mask = lax.broadcasted_iota(jnp.int32, (HALF, HALF), 1) <= lax.broadcasted_iota(jnp.int32, (HALF, HALF), 0)

    class Own:
        def __init__(self, h):
            self.h = h

        def q(self, rows=slice(None)):
            return q_scr[rows, self.h * HD : (self.h + 1) * HD]

        def state(self):
            return mx.at[self.h], acc.at[self.h]

    class Foreign:
        def __init__(self, f):
            self.f = f

        def q(self, rows=slice(None)):
            return fq[self.f, rows, :]

        def state(self):
            return fmx, facc

    def block(chip, kind, parity):
        rows = pl.ds(pl.multiple_of(parity * HALF, HALF), HALF)
        return jnp.concatenate([store[chip, kind, a, rows, :] for a in range(2)], axis=0)

    def chunk(chip, kind):
        return store[chip, kind].reshape(2 * TOK, HD)

    def causal(items, kb, vb):
        before = kb.shape[0] - TOK
        vb = with_ones(vb)
        for item in items:
            top, total = item.state()
            for part in range(2):
                rows = slice(part * HALF, (part + 1) * HALF)
                keys = before + (part + 1) * HALF
                s = qk(item.q(rows), kb[:keys])
                last = jnp.where(mask, s[:, keys - HALF :], NEG)
                s = last if keys == HALF else jnp.concatenate([s[:, : keys - HALF], last], axis=1)
                t = jnp.broadcast_to(jnp.max(s, axis=1, keepdims=True), (HALF, HD))
                top[rows, :] = t
                total[rows, :] = pv(jnp.exp2(s - wide(t, keys)), vb[:keys])

    def full(items, kb, vb):
        vb = with_ones(vb)
        for item in items:
            top, total = item.state()
            s = qk(item.q(), kb)
            old = top[...]
            new = jnp.maximum(old, jnp.max(s, axis=1, keepdims=True))
            factor = jnp.exp2(old - new)
            top[...] = new
            total[...] = total[...] * wide(factor, 2 * HD) + pv(jnp.exp2(s - wide(new, s.shape[1])), vb)

    own = [Own(h) for h in range(LH)]
    kept_heads = own[: LH - GIVEN]

    def on_own(condition, run):
        if GIVEN:
            pl.when(condition & home)(lambda: run(kept_heads))
            pl.when(condition & jnp.logical_not(home))(lambda: run(own))
        else:
            pl.when(condition)(lambda: run(own))

    on_own(c >= 0, lambda items: causal(items, block(y, 0, k), block(y, 1, k)))
    sends(1, start)

    def help_first():
        ask(0).wait_recv()
        fq[0] = (fq[0].astype(F32) * LOGIT).astype(BF)
        item = Foreign(0)

        @pl.when(k == 0)
        def _():
            causal(
                [item],
                jnp.concatenate([block(3, 0, 0), block(3, 0, 1)], axis=0),
                jnp.concatenate([block(3, 1, 0), block(3, 1, 1)], axis=0),
            )

        @pl.when(k == 1)
        def _():
            causal([item], block(3, 0, 0), block(3, 1, 0))

        for chip in (0, 1):
            full([item], chunk(chip, 0), chunk(chip, 1))

    near = y - 1
    two = (y == 3) | (helper & (GIVEN > 0))

    def step(j, carry):
        @pl.when((j == 0) & ((k == 1) | (helper & (GIVEN > 0))))
        def _():
            for a in range(2):
                over_core(y, 1 - k, a, wait_recv)

        @pl.when((j == 1) & (chunks > 0))
        def _():
            first(0, 0)

        @pl.when((j == 1) & two)
        def _():
            first(1, 0)

        @pl.when(j == 1)
        def _():
            passes(0)

        @pl.when((j == 1) & (chunks > 0))
        def _():
            third(0, 0)

        @pl.when((j == 2) & (chunks > 0))
        def _():
            first(0, 1)

        @pl.when((j == 2) & two)
        def _():
            first(1, 1)
            third(1, 0)

        @pl.when(j == 2)
        def _():
            passes(1)

        @pl.when((j == 3) & (chunks > 0))
        def _():
            third(0, 1)

        @pl.when((j == 4) & home)
        def _():
            for a in range(2):
                first(2, a)
            third(1, 1)

        if GIVEN:
            @pl.when((j == 4) & helper)
            def _():
                third(1, 1)
                help_first()
                for a in range(2):
                    first(2, a)

        chip = jnp.where(j == 0, y, jnp.where((j == 1) | (j == 3), near, 0))
        a_low = jnp.where(j >= 3, 1, 0)
        a_high = jnp.where(j == 0, 1, a_low)
        low = pl.ds(0, HALF)
        high = pl.ds(pl.multiple_of(jnp.where(j == 0, 0, HALF), HALF), HALF)

        def run(items):
            kb, vb = (
                jnp.concatenate([store[chip, kind, a_low, low, :], store[chip, kind, a_high, high, :]], axis=0)
                for kind in range(2)
            )
            full(items, kb, vb)

        on_own(
            ((j == 0) & (k == 1)) | (((j == 1) | (j == 3)) & (y > 0)) | (((j == 2) | (j == 4)) & (y == 3)), run
        )
        return carry

    lax.fori_loop(0, 5, step, 0)

    @pl.when(y == 2)
    def _():
        for a in range(2):
            first(1, a)
        for a in range(2):
            third(1, a)

    @pl.when(two)
    def _():
        for a in range(2):
            third(2, a)

    last = 3 - y + jnp.where(y == 3, 1, 0) - jnp.where(y == 2, 1, 0)
    on_own((y == 2) | (y == 3), lambda items: full(items, chunk(last, 0), chunk(last, 1)))

    row = lax.broadcasted_iota(jnp.int32, (TOK, HD), 0)

    def normal(total, position):
        o = total[:, :HD] / total[:, HD:]
        return jnp.where(row + position < length, o, 0.0).astype(BF)

    if GIVEN:
        @pl.when(helper)
        def _():
            full([Foreign(0)], chunk(2, 0), chunk(2, 1))
            fout[0] = normal(facc, (7 - c) * TOK)
            give_back(0).start()

    def finish(items):
        for item in items:
            out_ref[:, item.h * HD : (item.h + 1) * HD] = normal(acc.at[item.h], c * TOK)

    finish(kept_heads)
    if GIVEN:
        @pl.when(jnp.logical_not(home))
        def _():
            finish(own[LH - GIVEN :])

        @pl.when(home)
        def _():
            for f in range(GIVEN):
                give_back(f).wait_recv()

    asks(wait_send)
    for a in range(2):
        sends(a, wait_send)
    core_sends(wait_send)

    def done(i, carry):
        for a in range(2):
            forwards(i, a, wait_send)
        return carry

    lax.fori_loop(0, chunks, done, 0)

    if GIVEN:
        @pl.when(y == 1)
        def _():
            for a in range(2):
                over_y(2, a, left, 3, wait_send)

        @pl.when(helper)
        def _():
            for f in range(GIVEN):
                give_back(f).wait_send()


def hand_over(
    att_ref, pk_hbm, pv_hbm, owner_ref, layout_ref, length_ref,
    att, kc, vc, ks, vs,
    raw, made, b_ks, b_vs, att_sem, in_sem, out_sem,
):
    head = lax.axis_index("head")
    start = lax.axis_index("ctx") * TOK
    put = pltpu.make_async_copy(att_ref, att, att_sem)
    put.start()

    length = length_ref[0]
    found = jnp.int32(0)
    entry = [jnp.int32(0)] * SLOTS
    for r in range(KVH):
        kv = layout_ref[r]
        for i in range(PAGES):
            mine = owner_ref[i, 0, kv] == head
            for s in range(SLOTS):
                entry[s] = jnp.where(mine & (found == s), i * KVH + kv, entry[s])
            found = found + jnp.where(mine, 1, 0)
    gets = []
    for kind, source in enumerate((pk_hbm, pv_hbm)):
        for s in range(SLOTS):
            rows = pl.ds(pl.multiple_of((entry[s] >> 3) * PAGE, PAGE), PAGE)
            columns = pl.ds(pl.multiple_of((entry[s] & 7) * HD, HD), HD)
            gets.append(pltpu.make_async_copy(source.at[rows, columns], raw.at[kind, s], in_sem.at[kind, s]))
    for copy in gets:
        copy.start()
    rotation = signs()
    lanes = lax.broadcasted_iota(jnp.int32, (1, SLOTS), 1)
    page_row = lax.broadcasted_iota(jnp.int32, (PAGE, HD), 0)
    for copy in gets:
        copy.wait()
    puts = []
    for kind, (cache, scale_out, scale_scr) in enumerate(((kc, ks, b_ks), (vc, vs, b_vs))):
        kept = []
        for s in range(SLOTS):
            live = page_row + (start + (entry[s] >> 3) * PAGE) < length
            kept.append(jnp.where(live, raw[kind, s].astype(F32), 0.0).astype(BF))
        rotated = dot(jnp.concatenate(kept, axis=0), rotation, ((1,), (0,))) * (1.0 / math.sqrt(HD))
        rotated = rotated.reshape(SLOTS, PAGE, HD)
        largest = jnp.max(jnp.max(jnp.abs(rotated), axis=1, keepdims=True), axis=2, keepdims=True)
        scales = (largest / 448.0 + 1e-6).astype(BF).astype(F32)
        stored = rotated / scales
        scale_row = jnp.zeros((1, SLOTS), F32)
        for s in range(SLOTS):
            there = (jnp.zeros((1, 1), jnp.int32) + found) > s
            made[kind, s] = jnp.where(there, stored[s], 0.0).astype(BF)
            scale_row = jnp.where((lanes == s) & there, scales[s], scale_row)
        scale_scr[...] = scale_row.astype(BF)
        puts.append(pltpu.make_async_copy(made.at[kind], cache.at[0], out_sem.at[kind, 0]))
        puts.append(pltpu.make_async_copy(scale_scr, scale_out, out_sem.at[kind, 1]))
        for copy in puts[-2:]:
            copy.start()
    put.wait()
    for copy in puts:
        copy.wait()


def per_device(queries, prompt_keys, prompt_values, owner_map, head_layout, prompt_length):
    any_ = pl.BlockSpec(memory_space=pl.ANY)
    smem = pl.BlockSpec(memory_space=pltpu.SMEM)
    vmem = pl.BlockSpec(memory_space=pltpu.VMEM)
    dma = pltpu.SemaphoreType.DMA
    given = max(GIVEN, 1)
    attention = pl.pallas_call(
        kernel,
        out_shape=pltpu.VMEM((TOK, LH * HD), BF),
        in_specs=[any_, any_, any_, smem],
        out_specs=vmem,
        scratch_shapes=[
            pltpu.VMEM((TOK, LH * HD), BF),
            pltpu.VMEM((CHIPS, 2, 2, TOK, HD), BF),
            pltpu.VMEM((LH, TOK, 2 * HD), F32),
            pltpu.VMEM((LH, TOK, HD), F32),
            pltpu.VMEM((given, TOK, HD), BF),
            pltpu.VMEM((TOK, 2 * HD), F32),
            pltpu.VMEM((TOK, HD), F32),
            pltpu.VMEM((given, TOK, HD), BF),
            dma,
            dma((2, 2)),
            dma((4, 2, 2)),
            dma((CHIPS, 2, 2)),
            dma((CHIPS, 2, 2)),
            dma((CHIPS, 2, 2)),
            dma((given,)),
            dma((given,)),
            dma((given,)),
            dma((given,)),
        ],
        compiler_params=pltpu.CompilerParams(
            collective_id=0, has_side_effects=True, vmem_limit_bytes=56 << 20
        ),
        name="prefill",
    )(queries, prompt_keys, prompt_values, prompt_length)
    return pl.pallas_call(
        hand_over,
        out_shape=(
            jax.ShapeDtypeStruct((TOK, LH * HD), BF),
            jax.ShapeDtypeStruct((1, SLOTS, PAGE, HD), BF),
            jax.ShapeDtypeStruct((1, SLOTS, PAGE, HD), BF),
            jax.ShapeDtypeStruct((1, SLOTS), BF),
            jax.ShapeDtypeStruct((1, SLOTS), BF),
        ),
        in_specs=[vmem, any_, any_, smem, smem, smem],
        out_specs=(any_,) * 5,
        scratch_shapes=[
            pltpu.VMEM((2, SLOTS, PAGE, HD), BF),
            pltpu.VMEM((2, SLOTS, PAGE, HD), BF),
            pltpu.VMEM((1, SLOTS), BF),
            pltpu.VMEM((1, SLOTS), BF),
            dma,
            dma((2, SLOTS)),
            dma((2, 2)),
        ],
        compiler_params=pltpu.CompilerParams(vmem_limit_bytes=8 << 20),
        name="hand_over",
    )(attention, prompt_keys, prompt_values, owner_map.transpose(0, 2, 1), head_layout, prompt_length)


def solution(mesh):
    in_specs = (P("ctx", "head"), P("ctx", None), P("ctx", None), P("ctx", None, None), P(), P())
    out_specs = (
        P("ctx", "head"),
        P("ctx", "head", None, None),
        P("ctx", "head", None, None),
        P("ctx", "head"),
        P("ctx", "head"),
    )
    return jax.shard_map(
        per_device, mesh=mesh, in_specs=in_specs, out_specs=out_specs, check_vma=False
    )
```

```python
import math

import jax
import jax.numpy as jnp
from jax import lax
from jax.experimental import pallas as pl
from jax.experimental.pallas import tpu as pltpu
from jax.sharding import PartitionSpec as P

HD = 128
PAGE = 128
TOK = 512
LH = 8
KVH = 8
PAGES = 4
SLOTS = 4
CHIPS = 4
MESH = pl.DeviceIdType.MESH
HALF = TOK // 2
GIVEN = 1
BF = jnp.bfloat16
F32 = jnp.float32
NEG = -1e30
LOGIT = math.log2(math.e) / math.sqrt(HD)


def dot(a, b, dims):
    return lax.dot_general(a, b, (dims, ((), ())), preferred_element_type=F32)


def qk(q, k):
    return dot(q, k, ((1,), (1,)))


def pv(p, v):
    return dot(p.astype(BF), v, ((1,), (0,)))


def wide(x, columns):
    return jnp.tile(x, (1, columns // x.shape[1]))


def signs():
    row = lax.broadcasted_iota(jnp.int32, (HD, HD), 0)
    column = lax.broadcasted_iota(jnp.int32, (HD, HD), 1)
    common = row & column
    parity = common & 1
    for bit in range(1, 7):
        parity = parity ^ ((common >> bit) & 1)
    return (1 - 2 * parity).astype(F32).astype(BF)


def kernel(
    q_hbm, pk_hbm, pv_hbm, length_ref, out_ref,
    q_scr, store, acc, mx, fq, facc, fmx, fout,
    in_sem, own_sem, y_send, y_recv, s_send, s_recv, q_send, q_recv, o_send, o_recv,
):
    c = lax.axis_index("ctx")
    head = lax.axis_index("head")
    y = c // 2
    k = c % 2
    g = head // 2
    sib = {"ctx": 2 * y + (1 - k)}
    right = {"ctx": 2 * ((y + 1) % CHIPS) + k}
    left = {"ctx": 2 * ((y + CHIPS - 1) % CHIPS) + k}
    other_end = {"ctx": 7 - c}
    column = pl.ds(pl.multiple_of(g * HD, HD), HD)
    home = y == 3
    helper = y == 0
    inputs = (pk_hbm, pv_hbm)

    barrier = pltpu.get_barrier_semaphore()
    others = (sib, left, right, other_end) if GIVEN else (sib, left, right)
    for other in others:
        pl.semaphore_signal(barrier, inc=1, device_id=other, device_id_type=MESH)

    def piece(chip, parity, kind, a):
        return store.at[chip, kind, a, pl.ds(pl.multiple_of(parity * HALF, HALF), HALF), :]

    def raw(kind, a):
        return inputs[kind].at[pl.ds(a * HALF, HALF), column]

    def both(a):
        return ((0, a), (1, a))

    get_own = [
        pltpu.make_async_copy(raw(kind, a), piece(y, k, kind, a), own_sem.at[kind, a]) for a in range(2) for kind in range(2)
    ]
    get_q = pltpu.make_async_copy(q_hbm, q_scr, in_sem)
    for copy in (*get_own, get_q):
        copy.start()

    def remote(src, dst, send_sem, recv_sem, device):
        return pltpu.make_async_remote_copy(
            src_ref=src, dst_ref=dst, send_sem=send_sem, recv_sem=recv_sem, device_id=device, device_id_type=MESH
        )

    def own_over_y(a, device, place, act):
        for kind in range(2):
            ref = piece(y, k, kind, a)
            act(remote(ref, ref, y_send.at[place, kind, a], y_recv.at[y, kind, a], device))

    def over_y(chip, a, device, place, act):
        for kind in range(2):
            ref = piece(chip, k, kind, a)
            act(remote(ref, ref, y_send.at[place, kind, a], y_recv.at[chip, kind, a], device))

    def own_over_core(act):
        for a in range(2):
            for kind in range(2):
                ref = piece(y, k, kind, a)
                act(remote(ref, ref, s_send.at[y, kind, a], s_recv.at[y, kind, a], sib))

    def over_core(chip, parity, a, act):
        for kind in range(2):
            ref = piece(chip, parity, kind, a)
            act(remote(ref, ref, s_send.at[chip, kind, a], s_recv.at[chip, kind, a], sib))

    def ask(f):
        cols = pl.ds((LH - GIVEN + f) * HD, HD)
        return remote(q_hbm.at[:, cols], fq.at[f], q_send.at[f], q_recv.at[f], other_end)

    def give_back(part):
        rows = pl.ds(part * HALF, HALF)
        cols = pl.ds((LH - GIVEN) * HD, HD)
        return remote(fout.at[0, rows], out_ref.at[rows, cols], o_send.at[part], o_recv.at[part], other_end)

    def start(copy):
        copy.start()

    def wait_recv(copy):
        copy.wait_recv()

    def wait_send(copy):
        copy.wait_send()

    chunks = jnp.where(helper, CHIPS - 1 if GIVEN else 0, y)

    def source(i):
        return jnp.where(helper, jnp.where(i == 0, 1, jnp.where(i == 1, 3, 2)), jnp.where(i == 0, y - 1, i - 1))

    def sends(a, act):
        @pl.when(y < (4 if GIVEN else 3))
        def _():
            own_over_y(a, right, 0, act)

        @pl.when(y < (3 if GIVEN else 1))
        def _():
            own_over_y(a, left, 1, act)

    def asks(act):
        if GIVEN:
            @pl.when(home)
            def _():
                for f in range(GIVEN):
                    act(ask(f))

    def core_sends(act):
        @pl.when((k == 0) | (helper & (GIVEN > 0)))
        def _():
            own_over_core(act)

    def forwards(i, a, act):
        over_core(source(i), k, a, act)

        @pl.when((i == 0) & ((y == 1) | (y == 2)))
        def _():
            over_y(source(i), a, right, 2, act)

    def passes(a):
        if GIVEN:
            over_y(2, a, left, 3, wait_recv)
            over_y(2, a, left, 3, start)

    def first(i, a):
        over_y(source(i), a, right, 0, wait_recv)
        forwards(i, a, start)

    def third(i, a):
        over_core(source(i), 1 - k, a, wait_recv)

    pl.semaphore_wait(barrier, len(others))
    for copy in get_own:
        copy.wait()
    core_sends(start)
    sends(0, start)
    asks(start)

    length = length_ref[0]
    get_q.wait()
    q_scr[...] = (q_scr[...].astype(F32) * LOGIT).astype(BF)

    ones = jnp.ones((2 * TOK, HD), BF)

    def with_ones(v):
        return jnp.concatenate([v, ones[: v.shape[0]]], axis=1)

    mask = lax.broadcasted_iota(jnp.int32, (HALF, HALF), 1) <= lax.broadcasted_iota(jnp.int32, (HALF, HALF), 0)

    class Own:
        def __init__(self, h):
            self.h = h

        def q(self, rows=slice(None)):
            return q_scr[rows, self.h * HD : (self.h + 1) * HD]

        def state(self):
            return mx.at[self.h], acc.at[self.h]

    class ForeignPart:
        def __init__(self, rows):
            self.rows = rows

        def q(self):
            return fq[0, self.rows, :]

        def state(self):
            return fmx.at[self.rows], facc.at[self.rows]

    class Foreign:
        def __init__(self, f):
            self.f = f

        def q(self, rows=slice(None)):
            return fq[self.f, rows, :]

        def state(self):
            return fmx, facc

    def block(chip, kind, parity):
        rows = pl.ds(pl.multiple_of(parity * HALF, HALF), HALF)
        return jnp.concatenate([store[chip, kind, a, rows, :] for a in range(2)], axis=0)

    def chunk(chip, kind):
        return store[chip, kind].reshape(2 * TOK, HD)

    def causal(items, kb, vb):
        before = kb.shape[0] - TOK
        vb = with_ones(vb)
        for part in range(2):
            for item in items:
                top, total = item.state()
                rows = slice(part * HALF, (part + 1) * HALF)
                keys = before + (part + 1) * HALF
                s = qk(item.q(rows), kb[:keys])
                last = jnp.where(mask, s[:, keys - HALF :], NEG)
                s = last if keys == HALF else jnp.concatenate([s[:, : keys - HALF], last], axis=1)
                t = jnp.broadcast_to(jnp.max(s, axis=1, keepdims=True), (HALF, HD))
                top[rows, :] = t
                total[rows, :] = pv(jnp.exp2(s - wide(t, keys)), vb[:keys])

    def full(items, kb, vb):
        vb = with_ones(vb)
        for item in items:
            top, total = item.state()
            s = qk(item.q(), kb)
            old = top[...]
            new = jnp.maximum(old, jnp.max(s, axis=1, keepdims=True))
            factor = jnp.exp2(old - new)
            top[...] = new
            total[...] = total[...] * wide(factor, 2 * HD) + pv(jnp.exp2(s - wide(new, s.shape[1])), vb)

    own = [Own(h) for h in range(LH)]
    kept_heads = own[: LH - GIVEN]

    def on_own(condition, run):
        if GIVEN:
            pl.when(condition & home)(lambda: run(kept_heads))
            pl.when(condition & jnp.logical_not(home))(lambda: run(own))
        else:
            pl.when(condition)(lambda: run(own))

    on_own(c >= 0, lambda items: causal(items, block(y, 0, k), block(y, 1, k)))
    sends(1, start)

    def help_first():
        ask(0).wait_recv()
        fq[0] = (fq[0].astype(F32) * LOGIT).astype(BF)
        item = Foreign(0)

        @pl.when(k == 0)
        def _():
            causal(
                [item],
                jnp.concatenate([block(3, 0, 0), block(3, 0, 1)], axis=0),
                jnp.concatenate([block(3, 1, 0), block(3, 1, 1)], axis=0),
            )

        @pl.when(k == 1)
        def _():
            causal([item], block(3, 0, 0), block(3, 1, 0))

        for chip in (0, 1):
            full([item], chunk(chip, 0), chunk(chip, 1))

    near = y - 1
    two = (y == 3) | (helper & (GIVEN > 0))

    def step(j, carry):
        @pl.when((j == 0) & ((k == 1) | (helper & (GIVEN > 0))))
        def _():
            for a in range(2):
                over_core(y, 1 - k, a, wait_recv)

        @pl.when((j == 1) & (chunks > 0))
        def _():
            first(0, 0)

        @pl.when((j == 1) & two)
        def _():
            first(1, 0)

        @pl.when((j == 1) & (y == 1))
        def _():
            passes(0)
            first(0, 1)
            passes(1)

        @pl.when((j == 1) & (chunks > 0))
        def _():
            third(0, 0)

        @pl.when((j == 2) & (chunks > 0) & (y != 1))
        def _():
            first(0, 1)

        @pl.when((j == 2) & two)
        def _():
            first(1, 1)
            third(1, 0)

        @pl.when((j == 3) & (chunks > 0))
        def _():
            third(0, 1)

        @pl.when((j == 4) & home)
        def _():
            for a in range(2):
                first(2, a)
            third(1, 1)

        if GIVEN:
            @pl.when((j == 4) & helper)
            def _():
                third(1, 1)
                help_first()
                for a in range(2):
                    first(2, a)

        chip = jnp.where(j == 0, y, jnp.where((j == 1) | (j == 3), near, 0))
        a_low = jnp.where(j >= 3, 1, 0)
        a_high = jnp.where(j == 0, 1, a_low)
        low = pl.ds(0, HALF)
        high = pl.ds(pl.multiple_of(jnp.where(j == 0, 0, HALF), HALF), HALF)

        def run(items):
            kb, vb = (
                jnp.concatenate([store[chip, kind, a_low, low, :], store[chip, kind, a_high, high, :]], axis=0)
                for kind in range(2)
            )
            full(items, kb, vb)

        on_own(
            ((j == 0) & (k == 1)) | (((j == 1) | (j == 3)) & (y > 0)) | (((j == 2) | (j == 4)) & (y == 3)), run
        )
        return carry

    lax.fori_loop(0, 5, step, 0)

    @pl.when(y == 2)
    def _():
        for a in range(2):
            first(1, a)
        for a in range(2):
            third(1, a)

    @pl.when(two)
    def _():
        for a in range(2):
            third(2, a)

    last = 3 - y + jnp.where(y == 3, 1, 0) - jnp.where(y == 2, 1, 0)
    on_own((y == 2) | (y == 3), lambda items: full(items, chunk(last, 0), chunk(last, 1)))

    row = lax.broadcasted_iota(jnp.int32, (TOK, HD), 0)

    def normal(total, position):
        o = total[:, :HD] / total[:, HD:]
        return jnp.where(row[: o.shape[0]] + position < length, o, 0.0).astype(BF)

    if GIVEN:
        @pl.when(helper)
        def _():
            for part in range(2):
                rows = pl.ds(part * HALF, HALF)
                full([ForeignPart(rows)], chunk(2, 0), chunk(2, 1))
                fout[0, rows, :] = normal(facc.at[rows], (7 - c) * TOK + part * HALF)
                give_back(part).start()

    def finish(items):
        for item in items:
            out_ref[:, item.h * HD : (item.h + 1) * HD] = normal(acc.at[item.h], c * TOK)

    finish(kept_heads)
    if GIVEN:
        @pl.when(jnp.logical_not(home))
        def _():
            finish(own[LH - GIVEN :])

        @pl.when(home)
        def _():
            for part in range(2):
                give_back(part).wait_recv()

    asks(wait_send)
    for a in range(2):
        sends(a, wait_send)
    core_sends(wait_send)

    def done(i, carry):
        for a in range(2):
            forwards(i, a, wait_send)
        return carry

    lax.fori_loop(0, chunks, done, 0)

    if GIVEN:
        @pl.when(y == 1)
        def _():
            for a in range(2):
                over_y(2, a, left, 3, wait_send)

        @pl.when(helper)
        def _():
            for part in range(2):
                give_back(part).wait_send()


def hand_over(
    att_ref, pk_hbm, pv_hbm, owner_ref, layout_ref, length_ref,
    att, kc, vc, ks, vs,
    raw, made, b_ks, b_vs, att_sem, in_sem, out_sem,
):
    head = lax.axis_index("head")
    start = lax.axis_index("ctx") * TOK
    put = pltpu.make_async_copy(att_ref, att, att_sem)
    put.start()

    length = length_ref[0]
    found = jnp.int32(0)
    entry = [jnp.int32(0)] * SLOTS
    for r in range(KVH):
        kv = layout_ref[r]
        for i in range(PAGES):
            mine = owner_ref[i, 0, kv] == head
            for s in range(SLOTS):
                entry[s] = jnp.where(mine & (found == s), i * KVH + kv, entry[s])
            found = found + jnp.where(mine, 1, 0)
    gets = []
    for kind, source in enumerate((pk_hbm, pv_hbm)):
        for s in range(SLOTS):
            rows = pl.ds(pl.multiple_of((entry[s] >> 3) * PAGE, PAGE), PAGE)
            columns = pl.ds(pl.multiple_of((entry[s] & 7) * HD, HD), HD)
            gets.append(pltpu.make_async_copy(source.at[rows, columns], raw.at[kind, s], in_sem.at[kind, s]))
    for copy in gets:
        copy.start()
    rotation = signs()
    lanes = lax.broadcasted_iota(jnp.int32, (1, SLOTS), 1)
    page_row = lax.broadcasted_iota(jnp.int32, (PAGE, HD), 0)
    for copy in gets:
        copy.wait()
    puts = []
    for kind, (cache, scale_out, scale_scr) in enumerate(((kc, ks, b_ks), (vc, vs, b_vs))):
        kept = []
        for s in range(SLOTS):
            live = page_row + (start + (entry[s] >> 3) * PAGE) < length
            kept.append(jnp.where(live, raw[kind, s].astype(F32), 0.0).astype(BF))
        rotated = dot(jnp.concatenate(kept, axis=0), rotation, ((1,), (0,))) * (1.0 / math.sqrt(HD))
        rotated = rotated.reshape(SLOTS, PAGE, HD)
        largest = jnp.max(jnp.max(jnp.abs(rotated), axis=1, keepdims=True), axis=2, keepdims=True)
        scales = (largest / 448.0 + 1e-6).astype(BF).astype(F32)
        stored = rotated / scales
        scale_row = jnp.zeros((1, SLOTS), F32)
        for s in range(SLOTS):
            there = (jnp.zeros((1, 1), jnp.int32) + found) > s
            made[kind, s] = jnp.where(there, stored[s], 0.0).astype(BF)
            scale_row = jnp.where((lanes == s) & there, scales[s], scale_row)
        scale_scr[...] = scale_row.astype(BF)
        puts.append(pltpu.make_async_copy(made.at[kind], cache.at[0], out_sem.at[kind, 0]))
        puts.append(pltpu.make_async_copy(scale_scr, scale_out, out_sem.at[kind, 1]))
        for copy in puts[-2:]:
            copy.start()
    put.wait()
    for copy in puts:
        copy.wait()


def per_device(queries, prompt_keys, prompt_values, owner_map, head_layout, prompt_length):
    any_ = pl.BlockSpec(memory_space=pl.ANY)
    smem = pl.BlockSpec(memory_space=pltpu.SMEM)
    vmem = pl.BlockSpec(memory_space=pltpu.VMEM)
    dma = pltpu.SemaphoreType.DMA
    given = max(GIVEN, 1)
    attention = pl.pallas_call(
        kernel,
        out_shape=pltpu.VMEM((TOK, LH * HD), BF),
        in_specs=[any_, any_, any_, smem],
        out_specs=vmem,
        scratch_shapes=[
            pltpu.VMEM((TOK, LH * HD), BF),
            pltpu.VMEM((CHIPS, 2, 2, TOK, HD), BF),
            pltpu.VMEM((LH, TOK, 2 * HD), F32),
            pltpu.VMEM((LH, TOK, HD), F32),
            pltpu.VMEM((given, TOK, HD), BF),
            pltpu.VMEM((TOK, 2 * HD), F32),
            pltpu.VMEM((TOK, HD), F32),
            pltpu.VMEM((given, TOK, HD), BF),
            dma,
            dma((2, 2)),
            dma((4, 2, 2)),
            dma((CHIPS, 2, 2)),
            dma((CHIPS, 2, 2)),
            dma((CHIPS, 2, 2)),
            dma((given,)),
            dma((given,)),
            dma((2,)),
            dma((2,)),
        ],
        compiler_params=pltpu.CompilerParams(
            collective_id=0, has_side_effects=True, vmem_limit_bytes=56 << 20
        ),
        name="prefill",
    )(queries, prompt_keys, prompt_values, prompt_length)
    return pl.pallas_call(
        hand_over,
        out_shape=(
            jax.ShapeDtypeStruct((TOK, LH * HD), BF),
            jax.ShapeDtypeStruct((1, SLOTS, PAGE, HD), BF),
            jax.ShapeDtypeStruct((1, SLOTS, PAGE, HD), BF),
            jax.ShapeDtypeStruct((1, SLOTS), BF),
            jax.ShapeDtypeStruct((1, SLOTS), BF),
        ),
        in_specs=[vmem, any_, any_, smem, smem, smem],
        out_specs=(any_,) * 5,
        scratch_shapes=[
            pltpu.VMEM((2, SLOTS, PAGE, HD), BF),
            pltpu.VMEM((2, SLOTS, PAGE, HD), BF),
            pltpu.VMEM((1, SLOTS), BF),
            pltpu.VMEM((1, SLOTS), BF),
            dma,
            dma((2, SLOTS)),
            dma((2, 2)),
        ],
        compiler_params=pltpu.CompilerParams(vmem_limit_bytes=8 << 20),
        name="hand_over",
    )(attention, prompt_keys, prompt_values, owner_map.transpose(0, 2, 1), head_layout, prompt_length)


def solution(mesh):
    in_specs = (P("ctx", "head"), P("ctx", None), P("ctx", None), P("ctx", None, None), P(), P())
    out_specs = (
        P("ctx", "head"),
        P("ctx", "head", None, None),
        P("ctx", "head", None, None),
        P("ctx", "head"),
        P("ctx", "head"),
    )
    return jax.shard_map(
        per_device, mesh=mesh, in_specs=in_specs, out_specs=out_specs, check_vma=False
    )
```

```python
import math

import jax
import jax.numpy as jnp
from jax import lax
from jax.experimental import pallas as pl
from jax.experimental.pallas import tpu as pltpu
from jax.sharding import PartitionSpec as P

HD = 128
PAGE = 128
TOK = 512
LH = 8
KVH = 8
PAGES = 4
SLOTS = 4
CHIPS = 4
MESH = pl.DeviceIdType.MESH
HALF = TOK // 2
GIVEN = 1
BF = jnp.bfloat16
F32 = jnp.float32
NEG = -1e30
LOGIT = math.log2(math.e) / math.sqrt(HD)


def dot(a, b, dims):
    return lax.dot_general(a, b, (dims, ((), ())), preferred_element_type=F32)


def qk(q, k):
    return dot(q, k, ((1,), (1,)))


def pv(p, v):
    return dot(p.astype(BF), v, ((1,), (0,)))


def wide(x, columns):
    return jnp.tile(x, (1, columns // x.shape[1]))


def signs():
    row = lax.broadcasted_iota(jnp.int32, (HD, HD), 0)
    column = lax.broadcasted_iota(jnp.int32, (HD, HD), 1)
    common = row & column
    parity = common & 1
    for bit in range(1, 7):
        parity = parity ^ ((common >> bit) & 1)
    return (1 - 2 * parity).astype(F32).astype(BF)


def kernel(
    q_hbm, pk_hbm, pv_hbm, length_ref, out_ref,
    q_scr, store, acc, mx, fq, facc, fmx, fout,
    in_sem, own_sem, y_send, y_recv, s_send, s_recv, q_send, q_recv, o_send, o_recv,
):
    c = lax.axis_index("ctx")
    head = lax.axis_index("head")
    y = c // 2
    k = c % 2
    g = head // 2
    sib = {"ctx": 2 * y + (1 - k)}
    right = {"ctx": 2 * ((y + 1) % CHIPS) + k}
    left = {"ctx": 2 * ((y + CHIPS - 1) % CHIPS) + k}
    other_end = {"ctx": 7 - c}
    column = pl.ds(pl.multiple_of(g * HD, HD), HD)
    home = y == 3
    helper = y == 0
    inputs = (pk_hbm, pv_hbm)

    barrier = pltpu.get_barrier_semaphore()
    others = (sib, left, right, other_end) if GIVEN else (sib, left, right)
    for other in others:
        pl.semaphore_signal(barrier, inc=1, device_id=other, device_id_type=MESH)

    def piece(chip, parity, kind, a):
        return store.at[chip, kind, a, pl.ds(pl.multiple_of(parity * HALF, HALF), HALF), :]

    def raw(kind, a):
        return inputs[kind].at[pl.ds(a * HALF, HALF), column]

    def both(a):
        return ((0, a), (1, a))

    get_own = [
        pltpu.make_async_copy(raw(kind, a), piece(y, k, kind, a), own_sem.at[kind, a]) for a in range(2) for kind in range(2)
    ]
    get_q = pltpu.make_async_copy(q_hbm, q_scr, in_sem)
    for copy in (*get_own, get_q):
        copy.start()

    def remote(src, dst, send_sem, recv_sem, device):
        return pltpu.make_async_remote_copy(
            src_ref=src, dst_ref=dst, send_sem=send_sem, recv_sem=recv_sem, device_id=device, device_id_type=MESH
        )

    def own_over_y(a, device, place, act):
        for kind in range(2):
            ref = piece(y, k, kind, a)
            act(remote(ref, ref, y_send.at[place, kind, a], y_recv.at[y, kind, a], device))

    def over_y(chip, a, device, place, act):
        for kind in range(2):
            ref = piece(chip, k, kind, a)
            act(remote(ref, ref, y_send.at[place, kind, a], y_recv.at[chip, kind, a], device))

    def own_over_core(act):
        for a in range(2):
            for kind in range(2):
                ref = piece(y, k, kind, a)
                act(remote(ref, ref, s_send.at[y, kind, a], s_recv.at[y, kind, a], sib))

    def over_core(chip, parity, a, act):
        for kind in range(2):
            ref = piece(chip, parity, kind, a)
            act(remote(ref, ref, s_send.at[chip, kind, a], s_recv.at[chip, kind, a], sib))

    def ask(f):
        cols = pl.ds((LH - GIVEN + f) * HD, HD)
        return remote(q_hbm.at[:, cols], fq.at[f], q_send.at[f], q_recv.at[f], other_end)

    def give_back(part):
        rows = pl.ds(part * HALF, HALF)
        cols = pl.ds((LH - GIVEN) * HD, HD)
        return remote(fout.at[0, rows], out_ref.at[rows, cols], o_send.at[part], o_recv.at[part], other_end)

    def start(copy):
        copy.start()

    def wait_recv(copy):
        copy.wait_recv()

    def wait_send(copy):
        copy.wait_send()

    chunks = jnp.where(helper, CHIPS - 1 if GIVEN else 0, y)

    def source(i):
        return jnp.where(helper, jnp.where(i == 0, 1, jnp.where(i == 1, 3, 2)), jnp.where(i == 0, y - 1, i - 1))

    def sends(a, act):
        @pl.when(y < (4 if GIVEN else 3))
        def _():
            own_over_y(a, right, 0, act)

        @pl.when(y < (3 if GIVEN else 1))
        def _():
            own_over_y(a, left, 1, act)

    def asks(act):
        if GIVEN:
            @pl.when(home)
            def _():
                for f in range(GIVEN):
                    act(ask(f))

    def core_sends(act):
        @pl.when((k == 0) | (helper & (GIVEN > 0)))
        def _():
            own_over_core(act)

    def forwards(i, a, act):
        over_core(source(i), k, a, act)

        @pl.when((i == 0) & ((y == 1) | (y == 2)))
        def _():
            over_y(source(i), a, right, 2, act)

    def passes(a):
        if GIVEN:
            over_y(2, a, left, 3, wait_recv)
            over_y(2, a, left, 3, start)

    def first(i, a):
        over_y(source(i), a, right, 0, wait_recv)
        forwards(i, a, start)

    def third(i, a):
        over_core(source(i), 1 - k, a, wait_recv)

    pl.semaphore_wait(barrier, len(others))
    for copy in get_own:
        copy.wait()
    core_sends(start)
    sends(0, start)
    asks(start)

    length = length_ref[0]
    get_q.wait()
    q_scr[...] = (q_scr[...].astype(F32) * LOGIT).astype(BF)

    ones = jnp.ones((2 * TOK, HD), BF)

    def with_ones(v):
        return jnp.concatenate([v, ones[: v.shape[0]]], axis=1)

    mask = lax.broadcasted_iota(jnp.int32, (HALF, HALF), 1) <= lax.broadcasted_iota(jnp.int32, (HALF, HALF), 0)

    class Own:
        def __init__(self, h):
            self.h = h

        def q(self, rows=slice(None)):
            return q_scr[rows, self.h * HD : (self.h + 1) * HD]

        def state(self):
            return mx.at[self.h], acc.at[self.h]

    class ForeignPart:
        def __init__(self, rows):
            self.rows = rows

        def q(self):
            return fq[0, self.rows, :]

        def state(self):
            return fmx.at[self.rows], facc.at[self.rows]

    class Foreign:
        def __init__(self, f):
            self.f = f

        def q(self, rows=slice(None)):
            return fq[self.f, rows, :]

        def state(self):
            return fmx, facc

    def block(chip, kind, parity):
        rows = pl.ds(pl.multiple_of(parity * HALF, HALF), HALF)
        return jnp.concatenate([store[chip, kind, a, rows, :] for a in range(2)], axis=0)

    def chunk(chip, kind):
        return store[chip, kind].reshape(2 * TOK, HD)

    def causal(items, kb, vb):
        before = kb.shape[0] - TOK
        vb = with_ones(vb)
        for part in range(2):
            for item in items:
                top, total = item.state()
                rows = slice(part * HALF, (part + 1) * HALF)
                keys = before + (part + 1) * HALF
                s = qk(item.q(rows), kb[:keys])
                last = jnp.where(mask, s[:, keys - HALF :], NEG)
                s = last if keys == HALF else jnp.concatenate([s[:, : keys - HALF], last], axis=1)
                t = jnp.broadcast_to(jnp.max(s, axis=1, keepdims=True), (HALF, HD))
                top[rows, :] = t
                total[rows, :] = pv(jnp.exp2(s - wide(t, keys)), vb[:keys])

    def full(items, kb, vb):
        vb = with_ones(vb)
        for item in items:
            top, total = item.state()
            s = qk(item.q(), kb)
            old = top[...]
            new = jnp.maximum(old, jnp.max(s, axis=1, keepdims=True))
            factor = jnp.exp2(old - new)
            top[...] = new
            total[...] = total[...] * wide(factor, 2 * HD) + pv(jnp.exp2(s - wide(new, s.shape[1])), vb)

    own = [Own(h) for h in range(LH)]
    kept_heads = own[: LH - GIVEN]

    def on_own(condition, run):
        if GIVEN:
            pl.when(condition & home)(lambda: run(kept_heads))
            pl.when(condition & jnp.logical_not(home))(lambda: run(own))
        else:
            pl.when(condition)(lambda: run(own))

    on_own(c >= 0, lambda items: causal(items, block(y, 0, k), block(y, 1, k)))
    sends(1, start)

    def help_first():
        ask(0).wait_recv()
        fq[0] = (fq[0].astype(F32) * LOGIT).astype(BF)
        item = Foreign(0)

        @pl.when(k == 0)
        def _():
            causal(
                [item],
                jnp.concatenate([block(3, 0, 0), block(3, 0, 1)], axis=0),
                jnp.concatenate([block(3, 1, 0), block(3, 1, 1)], axis=0),
            )

        @pl.when(k == 1)
        def _():
            causal([item], block(3, 0, 0), block(3, 1, 0))

        for chip in (0, 1):
            full([item], chunk(chip, 0), chunk(chip, 1))

    near = y - 1
    two = (y == 3) | (helper & (GIVEN > 0))

    def step(j, carry):
        @pl.when((j == 0) & ((k == 1) | (helper & (GIVEN > 0))))
        def _():
            for a in range(2):
                over_core(y, 1 - k, a, wait_recv)

        @pl.when((j == 1) & (chunks > 0))
        def _():
            first(0, 0)

        @pl.when((j == 1) & two)
        def _():
            first(1, 0)

        @pl.when((j == 1) & (y == 1))
        def _():
            passes(0)
            first(0, 1)
            passes(1)

        @pl.when((j == 1) & (chunks > 0) & (y != 3))
        def _():
            third(0, 0)

        @pl.when((j == 2) & (chunks > 0) & (y != 1))
        def _():
            first(0, 1)

        @pl.when((j == 2) & two)
        def _():
            first(1, 1)
            third(1, 0)

        @pl.when((j == 2) & home)
        def _():
            third(0, 0)

        @pl.when((j == 3) & (chunks > 0) & (y != 3))
        def _():
            third(0, 1)

        @pl.when((j == 4) & home)
        def _():
            for a in range(2):
                first(2, a)
            third(0, 1)
            third(1, 1)

        if GIVEN:
            @pl.when((j == 4) & helper)
            def _():
                third(1, 1)
                help_first()
                for a in range(2):
                    first(2, a)

        spread = home & (j > 0)
        chip = jnp.where(j == 0, y, near)
        chip_high = jnp.where(spread, 0, chip)
        a_low = jnp.where(j >= 3, 1, 0)
        a_high = jnp.where(j == 0, 1, a_low)
        parity = jnp.where((j == 1) | (j == 3), k, 1 - k)
        low = pl.ds(pl.multiple_of(jnp.where(spread, parity, 0) * HALF, HALF), HALF)
        high = pl.ds(pl.multiple_of(jnp.where(spread, parity, jnp.where(j == 0, 0, 1)) * HALF, HALF), HALF)

        def run(items):
            kb, vb = (
                jnp.concatenate([store[chip, kind, a_low, low, :], store[chip_high, kind, a_high, high, :]], axis=0)
                for kind in range(2)
            )
            full(items, kb, vb)

        on_own(
            ((j == 0) & (k == 1)) | (((j == 1) | (j == 3)) & (y > 0)) | (((j == 2) | (j == 4)) & (y == 3)), run
        )
        return carry

    lax.fori_loop(0, 5, step, 0)

    @pl.when(y == 2)
    def _():
        for a in range(2):
            first(1, a)
        for a in range(2):
            third(1, a)

    @pl.when(two)
    def _():
        for a in range(2):
            third(2, a)

    last = 3 - y + jnp.where(y == 3, 1, 0) - jnp.where(y == 2, 1, 0)
    on_own((y == 2) | (y == 3), lambda items: full(items, chunk(last, 0), chunk(last, 1)))

    row = lax.broadcasted_iota(jnp.int32, (TOK, HD), 0)

    def normal(total, position):
        o = total[:, :HD] / total[:, HD:]
        return jnp.where(row[: o.shape[0]] + position < length, o, 0.0).astype(BF)

    if GIVEN:
        @pl.when(helper)
        def _():
            for part in range(2):
                rows = pl.ds(part * HALF, HALF)
                full([ForeignPart(rows)], chunk(2, 0), chunk(2, 1))
                fout[0, rows, :] = normal(facc.at[rows], (7 - c) * TOK + part * HALF)
                give_back(part).start()

    def finish(items):
        for item in items:
            out_ref[:, item.h * HD : (item.h + 1) * HD] = normal(acc.at[item.h], c * TOK)

    finish(kept_heads)
    if GIVEN:
        @pl.when(jnp.logical_not(home))
        def _():
            finish(own[LH - GIVEN :])

        @pl.when(home)
        def _():
            for part in range(2):
                give_back(part).wait_recv()

    asks(wait_send)
    for a in range(2):
        sends(a, wait_send)
    core_sends(wait_send)

    def done(i, carry):
        for a in range(2):
            forwards(i, a, wait_send)
        return carry

    lax.fori_loop(0, chunks, done, 0)

    if GIVEN:
        @pl.when(y == 1)
        def _():
            for a in range(2):
                over_y(2, a, left, 3, wait_send)

        @pl.when(helper)
        def _():
            for part in range(2):
                give_back(part).wait_send()


def hand_over(
    att_ref, pk_hbm, pv_hbm, owner_ref, layout_ref, length_ref,
    att, kc, vc, ks, vs,
    raw, made, b_ks, b_vs, att_sem, in_sem, out_sem,
):
    head = lax.axis_index("head")
    start = lax.axis_index("ctx") * TOK
    put = pltpu.make_async_copy(att_ref, att, att_sem)
    put.start()

    length = length_ref[0]
    found = jnp.int32(0)
    entry = [jnp.int32(0)] * SLOTS
    for r in range(KVH):
        kv = layout_ref[r]
        for i in range(PAGES):
            mine = owner_ref[i, 0, kv] == head
            for s in range(SLOTS):
                entry[s] = jnp.where(mine & (found == s), i * KVH + kv, entry[s])
            found = found + jnp.where(mine, 1, 0)
    gets = []
    for kind, source in enumerate((pk_hbm, pv_hbm)):
        for s in range(SLOTS):
            rows = pl.ds(pl.multiple_of((entry[s] >> 3) * PAGE, PAGE), PAGE)
            columns = pl.ds(pl.multiple_of((entry[s] & 7) * HD, HD), HD)
            gets.append(pltpu.make_async_copy(source.at[rows, columns], raw.at[kind, s], in_sem.at[kind, s]))
    for copy in gets:
        copy.start()
    rotation = signs()
    lanes = lax.broadcasted_iota(jnp.int32, (1, SLOTS), 1)
    page_row = lax.broadcasted_iota(jnp.int32, (PAGE, HD), 0)
    for copy in gets:
        copy.wait()
    puts = []
    for kind, (cache, scale_out, scale_scr) in enumerate(((kc, ks, b_ks), (vc, vs, b_vs))):
        kept = []
        for s in range(SLOTS):
            live = page_row + (start + (entry[s] >> 3) * PAGE) < length
            kept.append(jnp.where(live, raw[kind, s].astype(F32), 0.0).astype(BF))
        rotated = dot(jnp.concatenate(kept, axis=0), rotation, ((1,), (0,))) * (1.0 / math.sqrt(HD))
        rotated = rotated.reshape(SLOTS, PAGE, HD)
        largest = jnp.max(jnp.max(jnp.abs(rotated), axis=1, keepdims=True), axis=2, keepdims=True)
        scales = (largest / 448.0 + 1e-6).astype(BF).astype(F32)
        stored = rotated / scales
        scale_row = jnp.zeros((1, SLOTS), F32)
        for s in range(SLOTS):
            there = (jnp.zeros((1, 1), jnp.int32) + found) > s
            made[kind, s] = jnp.where(there, stored[s], 0.0).astype(BF)
            scale_row = jnp.where((lanes == s) & there, scales[s], scale_row)
        scale_scr[...] = scale_row.astype(BF)
        puts.append(pltpu.make_async_copy(made.at[kind], cache.at[0], out_sem.at[kind, 0]))
        puts.append(pltpu.make_async_copy(scale_scr, scale_out, out_sem.at[kind, 1]))
        for copy in puts[-2:]:
            copy.start()
    put.wait()
    for copy in puts:
        copy.wait()


def per_device(queries, prompt_keys, prompt_values, owner_map, head_layout, prompt_length):
    any_ = pl.BlockSpec(memory_space=pl.ANY)
    smem = pl.BlockSpec(memory_space=pltpu.SMEM)
    vmem = pl.BlockSpec(memory_space=pltpu.VMEM)
    dma = pltpu.SemaphoreType.DMA
    given = max(GIVEN, 1)
    attention = pl.pallas_call(
        kernel,
        out_shape=pltpu.VMEM((TOK, LH * HD), BF),
        in_specs=[any_, any_, any_, smem],
        out_specs=vmem,
        scratch_shapes=[
            pltpu.VMEM((TOK, LH * HD), BF),
            pltpu.VMEM((CHIPS, 2, 2, TOK, HD), BF),
            pltpu.VMEM((LH, TOK, 2 * HD), F32),
            pltpu.VMEM((LH, TOK, HD), F32),
            pltpu.VMEM((given, TOK, HD), BF),
            pltpu.VMEM((TOK, 2 * HD), F32),
            pltpu.VMEM((TOK, HD), F32),
            pltpu.VMEM((given, TOK, HD), BF),
            dma,
            dma((2, 2)),
            dma((4, 2, 2)),
            dma((CHIPS, 2, 2)),
            dma((CHIPS, 2, 2)),
            dma((CHIPS, 2, 2)),
            dma((given,)),
            dma((given,)),
            dma((2,)),
            dma((2,)),
        ],
        compiler_params=pltpu.CompilerParams(
            collective_id=0, has_side_effects=True, vmem_limit_bytes=56 << 20
        ),
        name="prefill",
    )(queries, prompt_keys, prompt_values, prompt_length)
    return pl.pallas_call(
        hand_over,
        out_shape=(
            jax.ShapeDtypeStruct((TOK, LH * HD), BF),
            jax.ShapeDtypeStruct((1, SLOTS, PAGE, HD), BF),
            jax.ShapeDtypeStruct((1, SLOTS, PAGE, HD), BF),
            jax.ShapeDtypeStruct((1, SLOTS), BF),
            jax.ShapeDtypeStruct((1, SLOTS), BF),
        ),
        in_specs=[vmem, any_, any_, smem, smem, smem],
        out_specs=(any_,) * 5,
        scratch_shapes=[
            pltpu.VMEM((2, SLOTS, PAGE, HD), BF),
            pltpu.VMEM((2, SLOTS, PAGE, HD), BF),
            pltpu.VMEM((1, SLOTS), BF),
            pltpu.VMEM((1, SLOTS), BF),
            dma,
            dma((2, SLOTS)),
            dma((2, 2)),
        ],
        compiler_params=pltpu.CompilerParams(vmem_limit_bytes=8 << 20),
        name="hand_over",
    )(attention, prompt_keys, prompt_values, owner_map.transpose(0, 2, 1), head_layout, prompt_length)


def solution(mesh):
    in_specs = (P("ctx", "head"), P("ctx", None), P("ctx", None), P("ctx", None, None), P(), P())
    out_specs = (
        P("ctx", "head"),
        P("ctx", "head", None, None),
        P("ctx", "head", None, None),
        P("ctx", "head"),
        P("ctx", "head"),
    )
    return jax.shard_map(
        per_device, mesh=mesh, in_specs=in_specs, out_specs=out_specs, check_vma=False
    )
```
